512 devices in a mesh: tgt: 16 (over x, y_lo, core), gz: 32 (over y_hi, z).
Axes of the slice: x: 4, y: 4 (y_hi: 2, y_lo: 2; y = y_hi * 2 + y_lo), z: 16, core: 2. Of those that a mesh axis runs over, the one named last changes fastest.
Arguments:
- flux: bfloat16 [512, 7808], P(('tgt', 'gz')), may hold values from -6 to 6
- ivar: bfloat16 [512, 7808], P(('tgt', 'gz')), may hold values from 0.099609375 to 10
- templates: bfloat16 [256, 10, 7808], P('gz', None, 'tgt'), may hold values from -0.08 to 0.08, as said below
- classes: int32 [512], P(('tgt', 'gz')), may hold values 0 or 1
Outputs:
- drop: float32 [512, 256], P(('tgt', 'gz'))
The draws below stay inside these ranges and needn't reach their ends.
Inputs may be any that keep to these rules, and one draw needn't show every extreme that they name: `templates`: every weighted Gram matrix is positive definite.
All inputs are finite; a program needn't handle non-finite values. No bound on the sum of `classes` on one device may be relied on, other than what follows from the above.
Results may differ from the reference program's by a relative error of at most 0.0018.
Values may be sent and summed in bfloat16 or wider, within the bound.
No kernel may reach another device: no remote copies, remote signals or barrier semaphores. Data moves between devices by JAX's collectives and lax.ppermute only.
A program may use at most 64 MiB of HBM per device.

```python
import math
import jax
import jax.numpy as jnp
from jax import lax

NPIX = 7808
K = 10
Z_DEV = 8
TARGETS = 512
Z = 256


def draw_templates(key, part):
    key = jax.random.fold_in(key, 7)
    first, second = jax.random.split(key)
    common = jnp.clip(jax.random.normal(first, (Z, 1, NPIX), jnp.float32), -5.0, 5.0)
    own = jnp.clip(jax.random.normal(second, (Z, K, NPIX), jnp.float32), -5.0, 5.0)
    values = (0.45 * common + 0.9 * own) * 0.0113
    return values.astype(jnp.bfloat16)


def place_ends(result, rng, low, high):
    longest = result.shape.index(max(result.shape))
    spots = []
    for shift in (0, 1):
        where = [jax.random.randint(jax.random.fold_in(rng, axis), (), 0, length) for axis, length in enumerate(result.shape)]
        where[longest] = (where[longest] + shift) % result.shape[longest]
        spots.append(tuple(where))
    return result.at[spots[0]].set(low).at[spots[1]].set(high)


def level_of(rng, dims, shards, least, top_value):
    def one(dim, shards_of):
        draws = jax.random.uniform(jax.random.fold_in(jax.random.fold_in(rng, 6), dim), (shards_of,), jnp.float32, least / len(shards), top_value / len(shards))
        return jnp.repeat(jnp.exp(draws), dims[dim] // shards_of).reshape((-1,) + (1,) * (len(dims) - dim - 1))

    level = one(*shards[0])
    for cut in shards[1:]:
        level = level * one(*cut)
    return level


def normal_values(own_key, dims, spread, limit, cuts=(), kind=jnp.bfloat16):
    result = spread * jax.random.normal(own_key, dims, jnp.float32)
    if cuts:
        result = result * level_of(own_key, dims, cuts, -0.22, 0.18)
    return jnp.clip(result, -limit, limit).astype(kind)


def setup_inputs(seed: int = 0) -> dict:
    key_list = jax.random.split(jax.random.key(seed), 5)
    return {
        "flux": normal_values(key_list[0], (TARGETS, NPIX), 1.0, 6.0, ((0, 512),)),
        "ivar": jnp.clip(jnp.exp(math.log(10.0) - 4.609084 * jax.random.uniform(key_list[1], (TARGETS, NPIX), jnp.float32) ** level_of(key_list[1], (TARGETS, NPIX), ((0, 512),), -0.2, 0.2)), 0.099609375, 10.0).astype(jnp.bfloat16),
        "templates": draw_templates(jax.random.fold_in(key_list[4], 71), 0),
        "classes": place_ends((jax.random.randint(key_list[3], (TARGETS,), 0, 3) < 1).astype(jnp.int32), jax.random.fold_in(key_list[3], 1), 0, 1),
    }


def pair_products(tmpl):
    wide = tmpl.astype(jnp.float32)
    count = wide.shape[1]
    pieces = [wide[:, k:k + 1, :] * wide[:, k:, :] for k in range(count)]
    return jnp.concatenate(pieces, axis=1).astype(jnp.bfloat16)

def solve_fit(gram, proj):
    count = proj.shape[-1]
    entries = jnp.moveaxis(gram, -1, 0)
    rights = jnp.moveaxis(proj, -1, 0)
    where = {}
    place = 0
    for k in range(count):
        for l in range(k, count):
            where[k, l] = place
            place = place + 1
    lower = {}
    for j in range(count):
        total = entries[where[j, j]]
        for m in range(j):
            total = total - lower[j, m] * lower[j, m]
        lower[j, j] = jnp.sqrt(total)
        for i in range(j + 1, count):
            value = entries[where[j, i]]
            for m in range(j):
                value = value - lower[i, m] * lower[j, m]
            lower[i, j] = value / lower[j, j]
    solved = []
    fit = jnp.zeros_like(rights[0])
    for i in range(count):
        value = rights[i]
        for m in range(i):
            value = value - lower[i, m] * solved[m]
        value = value / lower[i, i]
        solved.append(value)
        fit = fit + value * value
    return fit / count

def reference(flux, ivar, templates, classes):
    weighted = (ivar.astype(jnp.float32) * flux.astype(jnp.float32)).astype(jnp.bfloat16)
    weight_rows = weighted.astype(jnp.float32)
    ivar_rows = ivar.astype(jnp.float32)
    total_z = templates.shape[0]
    count = templates.shape[1]
    pixels = templates.shape[2]
    slab = Z_DEV
    blocks = templates.reshape(total_z // slab, slab, count, pixels)

    def block(tmpl):
        pairs = pair_products(tmpl).astype(jnp.float32).reshape(-1, pixels)
        gram = jnp.dot(ivar_rows, pairs.T, precision=lax.Precision.HIGHEST)
        proj = jnp.dot(weight_rows, tmpl.astype(jnp.float32).reshape(-1, pixels).T, precision=lax.Precision.HIGHEST)
        gram = gram.reshape(gram.shape[0], slab, -1)
        proj = proj.reshape(proj.shape[0], slab, count)
        return solve_fit(gram, proj)
    fits = lax.map(block, blocks)
    fit = jnp.transpose(fits, (1, 0, 2)).reshape(flux.shape[0], total_z)
    zindex = jnp.arange(total_z, dtype=jnp.int32)
    keep = (classes[:, None] == 1) | (zindex[None, :] < total_z * 3 // 10)
    return jnp.where(keep, fit, jnp.float32(0.0))
```

```python
import functools

import jax
import jax.numpy as jnp
from jax import lax
from jax.experimental import pallas as pl
from jax.experimental.pallas import tpu as pltpu
from jax.sharding import Mesh
from jax.sharding import PartitionSpec as P

BF16 = jnp.bfloat16
F32 = jnp.float32
LANES = 128
PAD = 512
TGT = ("x", "yl", "c")
GZ = ("yh", "z")
PLANE = ("x", "yl", "yh")
VMEM = pl.BlockSpec(memory_space=pltpu.VMEM)
SMEM = pl.BlockSpec(memory_space=pltpu.SMEM)
NT = (((1,), (1,)), ((), ()))


def pad16(n):
    return (n + 15) // 16 * 16


def strided(ref, start, size, stride):
    parts = [ref[j, pl.ds(start, size, stride=stride), :] for j in range(ref.shape[0])]
    return jnp.concatenate(parts, axis=1)


def prep_kernel(flux_ref, ivar_ref, tmpl_ref, rmsg_ref, tmsg_ref, rows, tmps):
    slab, count, width = tmpl_ref.shape
    chunks = rmsg_ref.shape[1] // 2
    rows[...] = jnp.zeros_like(rows)
    tmps[...] = jnp.zeros_like(tmps)
    ivar = ivar_ref[...].astype(F32)
    weighted = (ivar * flux_ref[...].astype(F32)).astype(BF16).astype(F32)
    for core in range(2):
        for which, value in enumerate((ivar, weighted)):
            for s in range(chunks):
                row = (core * 2 + which) * chunks + s
                start = (2 * s + core) * width
                rows[row : row + 1, 0:width] = value[:, start : start + width]
    rmsg_ref[...] = rows[...].reshape(rmsg_ref.shape).astype(BF16)
    step = pad16(count)
    for z in range(slab):
        value = tmpl_ref[z].astype(F32)
        for j in range(PAD // LANES):
            part = value[:, j * LANES : min((j + 1) * LANES, width)]
            tmps[j, z * step : z * step + count, 0 : part.shape[1]] = part
    for k in range(0, count, 2):
        both = [strided(tmps, k + i, slab, step) for i in range(2)]
        tile = jnp.concatenate(both, axis=0).astype(BF16)
        for copy in range(tmsg_ref.shape[0]):
            tmsg_ref[copy, k * slab : (k + 2) * slab, :] = tile


def gram_kernel(rows_ref, tmpl_ref, out_ref, rows, acc, *, slab, count):
    chunks = tmpl_ref.shape[0] // 2
    per = 2 * chunks
    nz = rows_ref.shape[0] // (2 * per)
    npairs = count * (count + 1) // 2
    for j in range(PAD // LANES):
        rows[j] = rows_ref[:, j * LANES : (j + 1) * LANES].astype(F32)
    for s in range(chunks):
        stat = []
        for which in range(2):
            cores = [
                strided(rows, core * per + which * chunks + s, nz, 2 * per)
                for core in range(2)
            ]
            stat.append(jnp.concatenate(cores, axis=0).astype(BF16))
        tk = []
        for k in range(count):
            halves = [
                tmpl_ref[2 * s + h, k * slab : (k + 1) * slab, :] for h in range(2)
            ]
            tk.append(jnp.concatenate(halves, axis=0))
        pairs = []
        for k in range(count):
            for l in range(k, count):
                pairs.append(
                    (tk[k].astype(F32) * tk[l].astype(F32)).astype(BF16)
                )
        gram = lax.dot_general(
            jnp.concatenate(pairs, axis=0), stat[0], NT, preferred_element_type=F32
        )
        proj = lax.dot_general(
            jnp.concatenate(tk, axis=0), stat[1], NT, preferred_element_type=F32
        )
        split = npairs * 2 * slab
        if s == 0:
            acc[0:split, :] = gram
            acc[split:, :] = proj
        else:
            acc[0:split, :] += gram
            acc[split:, :] += proj
    for e in range(npairs + count):
        for h in range(2):
            at = (2 * e + h) * slab
            out_ref[h, e * slab : (e + 1) * slab, :] = acc[at : at + slab, :]


def fit_kernel(part_ref, fit_ref, *, slab, count):
    npairs = count * (count + 1) // 2

    def entry(e):
        at = pl.ds(e * slab, slab)
        return part_ref[0, at, :] + part_ref[1, at, :]

    where = {}
    for k in range(count):
        for l in range(k, count):
            where[k, l] = len(where)
    lower = {}
    fit = None
    solved = []
    for j in range(count):
        total = entry(where[j, j])
        for m in range(j):
            total = total - lower[j, m] * lower[j, m]
        inv = lax.rsqrt(total)
        for i in range(j + 1, count):
            value = entry(where[j, i])
            for m in range(j):
                value = value - lower[i, m] * lower[j, m]
            lower[i, j] = value * inv
        value = entry(npairs + j)
        for m in range(j):
            value = value - lower[j, m] * solved[m]
        value = value * inv
        solved.append(value)
        fit = value * value if fit is None else fit + value * value
    fit_ref[...] = (fit / count).T


def drop_kernel(classes_ref, surface_ref, out_ref, *, galaxy_z):
    nsrc, slab = surface_ref.shape
    for i in range(nsrc):
        out_ref[:, i * slab : (i + 1) * slab] = surface_ref[i : i + 1, :]
    zindex = lax.broadcasted_iota(jnp.int32, out_ref.shape, 1)
    keep = (zindex < galaxy_z) | (classes_ref[0] == 1)
    out_ref[...] = jnp.where(keep, out_ref[...], 0.0)


def body(flux, ivar, templates, classes):
    slab, count, width = templates.shape
    entries = count * (count + 1) // 2 + count
    chunks = flux.shape[1] // width // 2
    rmsg, tmsg = pl.pallas_call(
        prep_kernel,
        out_shape=(
            jax.ShapeDtypeStruct((2, 2 * chunks, PAD), BF16),
            jax.ShapeDtypeStruct((2 * chunks, count * slab, PAD), BF16),
        ),
        in_specs=[VMEM] * 3,
        out_specs=(VMEM, VMEM),
        scratch_shapes=[
            pltpu.VMEM((4 * chunks, PAD), F32),
            pltpu.VMEM((PAD // LANES, slab * pad16(count), LANES), F32),
        ],
        name="prep",
    )(flux, ivar, templates)
    chip_rows = lax.all_gather(rmsg, "c", axis=0)
    mine = lax.dynamic_index_in_dim(chip_rows, lax.axis_index("c"), 1, keepdims=False)
    tmpl_all = lax.all_to_all(tmsg, PLANE, 0, 0, tiled=True)
    rows_all = lax.all_gather(mine, "z", axis=0)
    nz = rows_all.shape[0]
    part = pl.pallas_call(
        functools.partial(gram_kernel, slab=slab, count=count),
        out_shape=jax.ShapeDtypeStruct((2, entries * slab, 2 * nz), F32),
        in_specs=[VMEM] * 2,
        out_specs=VMEM,
        scratch_shapes=[
            pltpu.VMEM((PAD // LANES, nz * 4 * chunks, LANES), F32),
            pltpu.VMEM((entries * 2 * slab, 2 * nz), F32),
        ],
        compiler_params=pltpu.CompilerParams(vmem_limit_bytes=48 << 20),
        name="gram",
    )(rows_all.reshape(nz * 4 * chunks, PAD), tmpl_all)
    both = lax.all_to_all(part, "c", 0, 0, tiled=True)
    fit = pl.pallas_call(
        functools.partial(fit_kernel, slab=slab, count=count),
        out_shape=jax.ShapeDtypeStruct((2 * nz, slab), F32),
        in_specs=[VMEM],
        out_specs=VMEM,
        name="fit",
    )(both)
    surface = lax.all_to_all(fit, ("c", "z"), 0, 0, tiled=True)
    total_z = surface.shape[0] * slab
    return pl.pallas_call(
        functools.partial(drop_kernel, galaxy_z=total_z * 3 // 10),
        out_shape=jax.ShapeDtypeStruct((1, total_z), F32),
        in_specs=[SMEM, VMEM],
        out_specs=VMEM,
        name="drop",
    )(classes, surface)


def solution(mesh):
    fine = Mesh(mesh.devices.reshape(4, 2, 2, 2, 16), ("x", "yl", "c", "yh", "z"))
    return jax.shard_map(
        body,
        mesh=fine,
        in_specs=(
            P(TGT + GZ, None),
            P(TGT + GZ, None),
            P(GZ, None, TGT),
            P(TGT + GZ),
        ),
        out_specs=P(TGT + GZ, None),
        check_vma=False,
    )
```

```python
import functools

import jax
import jax.numpy as jnp
from jax import lax
from jax.experimental import pallas as pl
from jax.experimental.pallas import tpu as pltpu
from jax.sharding import Mesh
from jax.sharding import PartitionSpec as P

BF16 = jnp.bfloat16
F32 = jnp.float32
LANES = 128
PAD = 512
TGT = ("x", "yl", "c")
GZ = ("yh", "z")
PLANE = ("x", "yl", "yh")
VMEM = pl.BlockSpec(memory_space=pltpu.VMEM)
SMEM = pl.BlockSpec(memory_space=pltpu.SMEM)
NT = (((1,), (1,)), ((), ()))


def strided(ref, start, size, stride):
    parts = [ref[j, pl.ds(start, size, stride=stride), :] for j in range(ref.shape[0])]
    return jnp.concatenate(parts, axis=1)


def prep_kernel(classes_ref, flux_ref, ivar_ref, tmpl_ref, rmsg_ref, tmsg_ref, keep_ref, rows, *, galaxy_z):
    count, slab, width = tmpl_ref.shape
    chunks = rmsg_ref.shape[1] // 2
    rows[...] = jnp.zeros_like(rows)
    ivar = ivar_ref[...].astype(F32)
    weighted = (ivar * flux_ref[...].astype(F32)).astype(BF16).astype(F32)
    for core in range(2):
        for which, value in enumerate((ivar, weighted)):
            for s in range(chunks):
                row = (core * 2 + which) * chunks + s
                start = (2 * s + core) * width
                rows[row : row + 1, 0:width] = value[:, start : start + width]
    rmsg_ref[...] = rows[...].reshape(rmsg_ref.shape).astype(BF16)
    zeros = jnp.zeros((count * slab, PAD - width), BF16)
    tile = jnp.concatenate([tmpl_ref[...].reshape(count * slab, width), zeros], axis=1)
    for copy in range(tmsg_ref.shape[0]):
        tmsg_ref[copy] = tile
    zindex = lax.broadcasted_iota(jnp.int32, keep_ref.shape, 1)
    keep_ref[...] = jnp.where((zindex < galaxy_z) | (classes_ref[0] == 1), 1.0, 0.0)


def gram_kernel(rows_ref, tmpl_ref, out_ref, rows, acc, *, slab, count):
    chunks = tmpl_ref.shape[0] // 2
    per = 2 * chunks
    nz = rows_ref.shape[0] // (2 * per)
    npairs = count * (count + 1) // 2
    for j in range(PAD // LANES):
        rows[j] = rows_ref[:, j * LANES : (j + 1) * LANES].astype(F32)
    for s in range(chunks):
        stat = []
        for which in range(2):
            cores = [
                strided(rows, core * per + which * chunks + s, nz, 2 * per)
                for core in range(2)
            ]
            stat.append(jnp.concatenate(cores, axis=0).astype(BF16))
        tk = []
        for k in range(count):
            halves = [
                tmpl_ref[2 * s + h, k * slab : (k + 1) * slab, :] for h in range(2)
            ]
            tk.append(jnp.concatenate(halves, axis=0))
        pairs = []
        for k in range(count):
            for l in range(k, count):
                pairs.append(
                    (tk[k].astype(F32) * tk[l].astype(F32)).astype(BF16)
                )
        gram = lax.dot_general(
            jnp.concatenate(pairs, axis=0), stat[0], NT, preferred_element_type=F32
        )
        proj = lax.dot_general(
            jnp.concatenate(tk, axis=0), stat[1], NT, preferred_element_type=F32
        )
        split = npairs * 2 * slab
        if s == 0:
            acc[0:split, :] = gram
            acc[split:, :] = proj
        else:
            acc[0:split, :] += gram
            acc[split:, :] += proj
    entries = npairs + count
    ntarget = acc.shape[1]
    fold = LANES // ntarget
    for h in range(2):
        for g in range(out_ref.shape[1] // slab):
            parts = []
            for e in range(g * fold, (g + 1) * fold):
                at = (2 * min(e, entries - 1) + h) * slab
                parts.append(acc[at : at + slab, :])
            out_ref[h, g * slab : (g + 1) * slab, :] = jnp.concatenate(parts, axis=1)


def fit_kernel(part_ref, fit_ref, *, slab, count):
    npairs = count * (count + 1) // 2
    core = lax.axis_index("c")
    ntarget = fit_ref.shape[0]
    fold = LANES // ntarget
    sums = {}

    def entry(e):
        g = e // fold
        if g not in sums:
            at = pl.ds(g * slab, slab)
            sums[g] = part_ref[0, core, at, :] + part_ref[1, core, at, :]
        at = e % fold * ntarget
        return sums[g][:, at : at + ntarget]

    where = {}
    for k in range(count):
        for l in range(k, count):
            where[k, l] = len(where)
    lower = {}
    fit = None
    solved = []
    for j in range(count):
        total = entry(where[j, j])
        for m in range(j):
            total = total - lower[j, m] * lower[j, m]
        inv = lax.rsqrt(total)
        for i in range(j + 1, count):
            value = entry(where[j, i])
            for m in range(j):
                value = value - lower[i, m] * lower[j, m]
            lower[i, j] = value * inv
        value = entry(npairs + j)
        for m in range(j):
            value = value - lower[j, m] * solved[m]
        value = value * inv
        solved.append(value)
        fit = value * value if fit is None else fit + value * value
    fit_ref[...] = (fit / count).T


def drop_kernel(keep_ref, surface_ref, out_ref):
    nsrc, slab = surface_ref.shape
    for i in range(nsrc):
        at = slice(i * slab, (i + 1) * slab)
        value = surface_ref[i : i + 1, :]
        out_ref[:, at] = jnp.where(keep_ref[:, at] > 0.0, value, 0.0)


def body(flux, ivar, templates, classes):
    slab, count, width = templates.shape
    entries = count * (count + 1) // 2 + count
    chunks = flux.shape[1] // width // 2
    total_z = lax.axis_size(GZ) * slab
    fold = LANES // (2 * lax.axis_size("z"))
    groups = -(-entries // fold)
    rmsg, tmsg, keep = pl.pallas_call(
        functools.partial(prep_kernel, galaxy_z=total_z * 3 // 10),
        out_shape=(
            jax.ShapeDtypeStruct((2, 2 * chunks, PAD), BF16),
            jax.ShapeDtypeStruct((2 * chunks, count * slab, PAD), BF16),
            jax.ShapeDtypeStruct((1, total_z), F32),
        ),
        in_specs=[SMEM] + [VMEM] * 3,
        out_specs=(VMEM, VMEM, VMEM),
        scratch_shapes=[pltpu.VMEM((4 * chunks, PAD), F32)],
        name="prep",
    )(classes, flux, ivar, jnp.transpose(templates, (1, 0, 2)))
    chip_rows = lax.all_gather(rmsg, "c", axis=0)
    mine = lax.dynamic_index_in_dim(chip_rows, lax.axis_index("c"), 1, keepdims=False)
    tmpl_all = lax.all_to_all(tmsg, PLANE, 0, 0, tiled=True)
    rows_all = lax.all_gather(mine, "z", axis=0)
    nz = rows_all.shape[0]
    part = pl.pallas_call(
        functools.partial(gram_kernel, slab=slab, count=count),
        out_shape=jax.ShapeDtypeStruct((2, groups * slab, LANES), F32),
        in_specs=[VMEM] * 2,
        out_specs=VMEM,
        scratch_shapes=[
            pltpu.VMEM((PAD // LANES, nz * 4 * chunks, LANES), F32),
            pltpu.VMEM((entries * 2 * slab, 2 * nz), F32),
        ],
        compiler_params=pltpu.CompilerParams(vmem_limit_bytes=48 << 20),
        name="gram",
    )(rows_all.reshape(nz * 4 * chunks, PAD), tmpl_all)
    both = lax.all_gather(part, "c", axis=0)
    fit = pl.pallas_call(
        functools.partial(fit_kernel, slab=slab, count=count),
        out_shape=jax.ShapeDtypeStruct((2 * nz, slab), F32),
        in_specs=[VMEM],
        out_specs=VMEM,
        name="fit",
    )(both)
    surface = lax.all_to_all(fit, ("c", "z"), 0, 0, tiled=True)
    return pl.pallas_call(
        drop_kernel,
        out_shape=jax.ShapeDtypeStruct((1, total_z), F32),
        in_specs=[VMEM, VMEM],
        out_specs=VMEM,
        name="drop",
    )(keep, surface)


def solution(mesh):
    fine = Mesh(mesh.devices.reshape(4, 2, 2, 2, 16), ("x", "yl", "c", "yh", "z"))
    return jax.shard_map(
        body,
        mesh=fine,
        in_specs=(
            P(TGT + GZ, None),
            P(TGT + GZ, None),
            P(GZ, None, TGT),
            P(TGT + GZ),
        ),
        out_specs=P(TGT + GZ, None),
        check_vma=False,
    )
```

```python
import functools

import jax
import jax.numpy as jnp
from jax import lax
from jax.experimental import pallas as pl
from jax.experimental.pallas import tpu as pltpu
from jax.sharding import Mesh
from jax.sharding import PartitionSpec as P

BF16 = jnp.bfloat16
F32 = jnp.float32
LANES = 128
PAD = 512
TGT = ("x", "yl", "c")
GZ = ("yh", "z")
PLANE = ("x", "yl", "yh")
VMEM = pl.BlockSpec(memory_space=pltpu.VMEM)
SMEM = pl.BlockSpec(memory_space=pltpu.SMEM)
NT = (((1,), (1,)), ((), ()))


def in_hbm(x):
    return pltpu.with_memory_space_constraint(x, pltpu.HBM)


def in_vmem(x):
    return pltpu.with_memory_space_constraint(x, pltpu.VMEM)


def strided(ref, start, size, stride):
    parts = [ref[j, pl.ds(start, size, stride=stride), :] for j in range(ref.shape[0])]
    return jnp.concatenate(parts, axis=1)


def prep_kernel(classes_ref, flux_ref, ivar_ref, tmpl_ref, rmsg_ref, tmsg_ref, keep_ref, rows, *, galaxy_z):
    count, slab, width = tmpl_ref.shape
    chunks = rmsg_ref.shape[1] // 2
    rows[...] = jnp.zeros_like(rows)
    ivar = ivar_ref[...].astype(F32)
    weighted = (ivar * flux_ref[...].astype(F32)).astype(BF16).astype(F32)
    for core in range(2):
        for which, value in enumerate((ivar, weighted)):
            for s in range(chunks):
                row = (core * 2 + which) * chunks + s
                start = (2 * s + core) * width
                rows[row : row + 1, 0:width] = value[:, start : start + width]
    rmsg_ref[...] = rows[...].reshape(rmsg_ref.shape).astype(BF16)
    zeros = jnp.zeros((count * slab, PAD - width), BF16)
    tile = jnp.concatenate([tmpl_ref[...].reshape(count * slab, width), zeros], axis=1)
    for copy in range(tmsg_ref.shape[0]):
        tmsg_ref[copy] = tile
    zindex = lax.broadcasted_iota(jnp.int32, keep_ref.shape, 1)
    keep_ref[...] = jnp.where((zindex < galaxy_z) | (classes_ref[0] == 1), 1.0, 0.0)


def gram_kernel(rows_ref, tmpl_ref, out_ref, rows, acc, *, slab, count):
    chunks = tmpl_ref.shape[0] // 2
    per = 2 * chunks
    nz = rows_ref.shape[0] // (2 * per)
    npairs = count * (count + 1) // 2
    for j in range(PAD // LANES):
        rows[j] = rows_ref[:, j * LANES : (j + 1) * LANES].astype(F32)
    for s in range(chunks):
        stat = []
        for which in range(2):
            cores = [
                strided(rows, core * per + which * chunks + s, nz, 2 * per)
                for core in range(2)
            ]
            stat.append(jnp.concatenate(cores, axis=0).astype(BF16))
        tk = []
        for k in range(count):
            halves = [
                tmpl_ref[2 * s + h, k * slab : (k + 1) * slab, :] for h in range(2)
            ]
            tk.append(jnp.concatenate(halves, axis=0))
        pairs = []
        for k in range(count):
            for l in range(k, count):
                pairs.append(
                    (tk[k].astype(F32) * tk[l].astype(F32)).astype(BF16)
                )
        gram = lax.dot_general(
            jnp.concatenate(pairs, axis=0), stat[0], NT, preferred_element_type=F32
        )
        proj = lax.dot_general(
            jnp.concatenate(tk, axis=0), stat[1], NT, preferred_element_type=F32
        )
        split = npairs * 2 * slab
        if s == 0:
            acc[0:split, :] = gram
            acc[split:, :] = proj
        else:
            acc[0:split, :] += gram
            acc[split:, :] += proj
    entries = npairs + count
    ntarget = acc.shape[1]
    fold = LANES // ntarget
    for h in range(2):
        for g in range(out_ref.shape[1] // slab):
            parts = []
            for e in range(g * fold, (g + 1) * fold):
                at = (2 * min(e, entries - 1) + h) * slab
                parts.append(acc[at : at + slab, :])
            out_ref[h, g * slab : (g + 1) * slab, :] = jnp.concatenate(parts, axis=1)


def fit_kernel(part_ref, fit_ref, *, slab, count):
    npairs = count * (count + 1) // 2
    core = lax.axis_index("c")
    ntarget = fit_ref.shape[0]
    fold = LANES // ntarget
    sums = {}

    def entry(e):
        g = e // fold
        if g not in sums:
            at = pl.ds(g * slab, slab)
            sums[g] = part_ref[0, core, at, :] + part_ref[1, core, at, :]
        at = e % fold * ntarget
        return sums[g][:, at : at + ntarget]

    where = {}
    for k in range(count):
        for l in range(k, count):
            where[k, l] = len(where)
    lower = {}
    fit = None
    solved = []
    for j in range(count):
        total = entry(where[j, j])
        for m in range(j):
            total = total - lower[j, m] * lower[j, m]
        inv = lax.rsqrt(total)
        for i in range(j + 1, count):
            value = entry(where[j, i])
            for m in range(j):
                value = value - lower[i, m] * lower[j, m]
            lower[i, j] = value * inv
        value = entry(npairs + j)
        for m in range(j):
            value = value - lower[j, m] * solved[m]
        value = value * inv
        solved.append(value)
        fit = value * value if fit is None else fit + value * value
    fit_ref[...] = (fit / count).T


def drop_kernel(keep_ref, surface_ref, out_ref):
    nsrc, slab = surface_ref.shape
    for i in range(nsrc):
        at = slice(i * slab, (i + 1) * slab)
        value = surface_ref[i : i + 1, :]
        out_ref[:, at] = jnp.where(keep_ref[:, at] > 0.0, value, 0.0)


def body(flux, ivar, templates, classes):
    slab, count, width = templates.shape
    entries = count * (count + 1) // 2 + count
    chunks = flux.shape[1] // width // 2
    total_z = lax.axis_size(GZ) * slab
    fold = LANES // (2 * lax.axis_size("z"))
    groups = -(-entries // fold)
    rmsg, tmsg, keep = pl.pallas_call(
        functools.partial(prep_kernel, galaxy_z=total_z * 3 // 10),
        out_shape=(
            pltpu.VMEM((2, 2 * chunks, PAD), BF16),
            pltpu.VMEM((2 * chunks, count * slab, PAD), BF16),
            jax.ShapeDtypeStruct((1, total_z), F32),
        ),
        in_specs=[SMEM] + [VMEM] * 3,
        out_specs=(VMEM, VMEM, VMEM),
        scratch_shapes=[pltpu.VMEM((4 * chunks, PAD), F32)],
        compiler_params=pltpu.CompilerParams(vmem_limit_bytes=8 << 20),
        name="prep",
    )(classes, in_hbm(flux), in_hbm(ivar), in_hbm(jnp.transpose(templates, (1, 0, 2))))
    chip_rows = lax.all_gather(rmsg, "c", axis=0)
    mine = lax.dynamic_index_in_dim(chip_rows, lax.axis_index("c"), 1, keepdims=False)
    tmpl_all = lax.all_to_all(tmsg, PLANE, 0, 0, tiled=True)
    rows_all = lax.all_gather(mine, "z", axis=0)
    nz = rows_all.shape[0]
    part = pl.pallas_call(
        functools.partial(gram_kernel, slab=slab, count=count),
        out_shape=pltpu.VMEM((2, groups * slab, LANES), F32),
        in_specs=[VMEM] * 2,
        out_specs=VMEM,
        scratch_shapes=[
            pltpu.VMEM((PAD // LANES, nz * 4 * chunks, LANES), F32),
            pltpu.VMEM((entries * 2 * slab, 2 * nz), F32),
        ],
        compiler_params=pltpu.CompilerParams(vmem_limit_bytes=16 << 20),
        name="gram",
    )(rows_all.reshape(nz * 4 * chunks, PAD), tmpl_all)
    both = lax.all_gather(part, "c", axis=0)
    fit = pl.pallas_call(
        functools.partial(fit_kernel, slab=slab, count=count),
        out_shape=pltpu.VMEM((2 * nz, slab), F32),
        in_specs=[VMEM],
        out_specs=VMEM,
        compiler_params=pltpu.CompilerParams(vmem_limit_bytes=4 << 20),
        name="fit",
    )(in_vmem(both))
    surface = lax.all_to_all(fit, ("c", "z"), 0, 0, tiled=True)
    return pl.pallas_call(
        drop_kernel,
        out_shape=jax.ShapeDtypeStruct((1, total_z), F32),
        in_specs=[VMEM, VMEM],
        out_specs=VMEM,
        compiler_params=pltpu.CompilerParams(vmem_limit_bytes=4 << 20),
        name="drop",
    )(in_vmem(keep), in_vmem(surface))


def solution(mesh):
    fine = Mesh(mesh.devices.reshape(4, 2, 2, 2, 16), ("x", "yl", "c", "yh", "z"))
    return jax.shard_map(
        body,
        mesh=fine,
        in_specs=(
            P(TGT + GZ, None),
            P(TGT + GZ, None),
            P(GZ, None, TGT),
            P(TGT + GZ),
        ),
        out_specs=P(TGT + GZ, None),
        check_vma=False,
    )
```

```python
import functools

import jax
import jax.numpy as jnp
from jax import lax
from jax.experimental import pallas as pl
from jax.experimental.pallas import tpu as pltpu
from jax.sharding import Mesh
from jax.sharding import PartitionSpec as P

BF16 = jnp.bfloat16
F32 = jnp.float32
LANES = 128
PAD = 512
TGT = ("x", "yl", "c")
GZ = ("yh", "z")
PLANE = ("x", "yl", "yh")
VMEM = pl.BlockSpec(memory_space=pltpu.VMEM)
SMEM = pl.BlockSpec(memory_space=pltpu.SMEM)
NT = (((1,), (1,)), ((), ()))


def in_hbm(x):
    return pltpu.with_memory_space_constraint(x, pltpu.HBM)


def in_vmem(x):
    return pltpu.with_memory_space_constraint(x, pltpu.VMEM)


def strided(ref, start, size, stride):
    parts = [ref[j, pl.ds(start, size, stride=stride), :] for j in range(ref.shape[0])]
    return jnp.concatenate(parts, axis=1)


def prep_kernel(classes_ref, flux_ref, ivar_ref, tmpl_ref, rmsg_ref, tmsg_ref, keep_ref, rows, *, galaxy_z):
    count, slab, width = tmpl_ref.shape
    chunks = rmsg_ref.shape[0] // 4
    ivar = ivar_ref[...].astype(F32)
    weighted = (ivar * flux_ref[...].astype(F32)).astype(BF16).astype(F32)
    for core in range(2):
        for which, value in enumerate((ivar, weighted)):
            for s in range(chunks):
                row = (core * 2 + which) * chunks + s
                start = (2 * s + core) * width
                rows[row : row + 1, :] = value[:, start : start + width]
    rmsg_ref[...] = rows[...].astype(BF16)
    zeros = jnp.zeros((count * slab, PAD - width), BF16)
    tile = jnp.concatenate([tmpl_ref[...].reshape(count * slab, width), zeros], axis=1)
    for copy in range(tmsg_ref.shape[0]):
        tmsg_ref[copy] = tile
    zindex = lax.broadcasted_iota(jnp.int32, keep_ref.shape, 1)
    keep_ref[...] = jnp.where((zindex < galaxy_z) | (classes_ref[0] == 1), 1.0, 0.0)


def gram_kernel(rows_ref, tmpl_ref, out_ref, rows, acc, *, slab, count):
    chunks = tmpl_ref.shape[0] // 2
    per = 2 * chunks
    nz, width = rows_ref.shape[1], rows_ref.shape[3]
    npairs = count * (count + 1) // 2
    core, z = lax.axis_index("c"), lax.axis_index("z")
    last = PAD // LANES - 1
    rows[last] = jnp.zeros_like(rows[last])
    for j in range(2):
        for other in range(nz):
            block = rows_ref[j, other, pl.ds(core * per, per), :].astype(F32)
            owner = lax.rem(j + z + other, 2)
            at = pl.ds((owner * nz + other) * per, per)
            for i in range(last + 1):
                part = block[:, i * LANES : min((i + 1) * LANES, width)]
                rows[i, at, 0 : part.shape[1]] = part
    for s in range(chunks):
        stat = []
        for which in range(2):
            value = strided(rows, which * chunks + s, 2 * nz, per)
            stat.append(value.astype(BF16))
        tk = []
        for k in range(count):
            halves = [
                tmpl_ref[2 * s + h, k * slab : (k + 1) * slab, :] for h in range(2)
            ]
            tk.append(jnp.concatenate(halves, axis=0))
        pairs = []
        for k in range(count):
            for l in range(k, count):
                pairs.append(
                    (tk[k].astype(F32) * tk[l].astype(F32)).astype(BF16)
                )
        gram = lax.dot_general(
            jnp.concatenate(pairs, axis=0), stat[0], NT, preferred_element_type=F32
        )
        proj = lax.dot_general(
            jnp.concatenate(tk, axis=0), stat[1], NT, preferred_element_type=F32
        )
        split = npairs * 2 * slab
        if s == 0:
            acc[0:split, :] = gram
            acc[split:, :] = proj
        else:
            acc[0:split, :] += gram
            acc[split:, :] += proj
    entries = npairs + count
    ntarget = acc.shape[1]
    fold = LANES // ntarget
    for h in range(2):
        for g in range(out_ref.shape[1] // slab):
            parts = []
            for e in range(g * fold, (g + 1) * fold):
                at = (2 * min(e, entries - 1) + h) * slab
                parts.append(acc[at : at + slab, :])
            out_ref[h, g * slab : (g + 1) * slab, :] = jnp.concatenate(parts, axis=1)


def fit_kernel(part_ref, fit_ref, *, slab, count):
    npairs = count * (count + 1) // 2
    core = lax.axis_index("c")
    ntarget = fit_ref.shape[0]
    fold = LANES // ntarget
    sums = {}

    def entry(e):
        g = e // fold
        if g not in sums:
            at = pl.ds(g * slab, slab)
            sums[g] = part_ref[0, core, at, :] + part_ref[1, core, at, :]
        at = e % fold * ntarget
        return sums[g][:, at : at + ntarget]

    where = {}
    for k in range(count):
        for l in range(k, count):
            where[k, l] = len(where)
    lower = {}
    fit = None
    solved = []
    for j in range(count):
        total = entry(where[j, j])
        for m in range(j):
            total = total - lower[j, m] * lower[j, m]
        inv = lax.rsqrt(total)
        for i in range(j + 1, count):
            value = entry(where[j, i])
            for m in range(j):
                value = value - lower[i, m] * lower[j, m]
            lower[i, j] = value * inv
        value = entry(npairs + j)
        for m in range(j):
            value = value - lower[j, m] * solved[m]
        value = value * inv
        solved.append(value)
        fit = value * value if fit is None else fit + value * value
    fit_ref[...] = (fit / count).T


def drop_kernel(keep_ref, surface_ref, out_ref):
    nsrc, slab = surface_ref.shape
    for i in range(nsrc):
        at = slice(i * slab, (i + 1) * slab)
        value = surface_ref[i : i + 1, :]
        out_ref[:, at] = jnp.where(keep_ref[:, at] > 0.0, value, 0.0)


def body(flux, ivar, templates, classes):
    slab, count, width = templates.shape
    entries = count * (count + 1) // 2 + count
    chunks = flux.shape[1] // width // 2
    total_z = lax.axis_size(GZ) * slab
    fold = LANES // (2 * lax.axis_size("z"))
    groups = -(-entries // fold)
    rmsg, tmsg, keep = pl.pallas_call(
        functools.partial(prep_kernel, galaxy_z=total_z * 3 // 10),
        out_shape=(
            pltpu.VMEM((2 * 2 * chunks, width), BF16),
            pltpu.VMEM((2 * chunks, count * slab, PAD), BF16),
            jax.ShapeDtypeStruct((1, total_z), F32),
        ),
        in_specs=[SMEM] + [VMEM] * 3,
        out_specs=(VMEM, VMEM, VMEM),
        scratch_shapes=[pltpu.VMEM((4 * chunks, width), F32)],
        compiler_params=pltpu.CompilerParams(vmem_limit_bytes=8 << 20),
        name="prep",
    )(classes, in_hbm(flux), in_hbm(ivar), in_hbm(jnp.transpose(templates, (1, 0, 2))))
    tmpl_all = lax.all_to_all(tmsg, PLANE, 0, 0, tiled=True)
    nz = lax.axis_size("z")
    rings = [[(g + z) % 2 * nz + z for z in range(nz)] for g in range(2)]
    ring_rows = lax.all_gather(rmsg, ("c", "z"), axis=0, axis_index_groups=rings)
    rows_all = lax.all_gather(ring_rows, "c", axis=0)
    part = pl.pallas_call(
        functools.partial(gram_kernel, slab=slab, count=count),
        out_shape=pltpu.VMEM((2, groups * slab, LANES), F32),
        in_specs=[VMEM] * 2,
        out_specs=VMEM,
        scratch_shapes=[
            pltpu.VMEM((PAD // LANES, 2 * nz * 2 * chunks, LANES), F32),
            pltpu.VMEM((entries * 2 * slab, 2 * nz), F32),
        ],
        compiler_params=pltpu.CompilerParams(vmem_limit_bytes=16 << 20),
        name="gram",
    )(in_vmem(rows_all), tmpl_all)
    both = lax.all_gather(part, "c", axis=0)
    fit = pl.pallas_call(
        functools.partial(fit_kernel, slab=slab, count=count),
        out_shape=pltpu.VMEM((2 * nz, slab), F32),
        in_specs=[VMEM],
        out_specs=VMEM,
        compiler_params=pltpu.CompilerParams(vmem_limit_bytes=4 << 20),
        name="fit",
    )(in_vmem(both))
    surface = lax.all_to_all(fit, ("c", "z"), 0, 0, tiled=True)
    return pl.pallas_call(
        drop_kernel,
        out_shape=jax.ShapeDtypeStruct((1, total_z), F32),
        in_specs=[VMEM, VMEM],
        out_specs=VMEM,
        compiler_params=pltpu.CompilerParams(vmem_limit_bytes=4 << 20),
        name="drop",
    )(in_vmem(keep), in_vmem(surface))


def solution(mesh):
    fine = Mesh(mesh.devices.reshape(4, 2, 2, 2, 16), ("x", "yl", "c", "yh", "z"))
    return jax.shard_map(
        body,
        mesh=fine,
        in_specs=(
            P(TGT + GZ, None),
            P(TGT + GZ, None),
            P(GZ, None, TGT),
            P(TGT + GZ),
        ),
        out_specs=P(TGT + GZ, None),
        check_vma=False,
    )
```

```python
import functools

import jax
import jax.numpy as jnp
from jax import lax
from jax.experimental import pallas as pl
from jax.experimental.pallas import tpu as pltpu
from jax.sharding import Mesh
from jax.sharding import PartitionSpec as P

BF16 = jnp.bfloat16
F32 = jnp.float32
LANES = 128
PAD = 512
TGT = ("x", "yl", "c")
GZ = ("yh", "z")
PLANE = ("x", "yl", "yh")
VMEM = pl.BlockSpec(memory_space=pltpu.VMEM)
SMEM = pl.BlockSpec(memory_space=pltpu.SMEM)
NT = (((1,), (1,)), ((), ()))


def in_hbm(x):
    return pltpu.with_memory_space_constraint(x, pltpu.HBM)


def in_vmem(x):
    return pltpu.with_memory_space_constraint(x, pltpu.VMEM)


def strided(ref, start, size, stride):
    parts = [ref[j, pl.ds(start, size, stride=stride), :] for j in range(ref.shape[0])]
    return jnp.concatenate(parts, axis=1)


def prep_kernel(classes_ref, flux_ref, ivar_ref, tmpl_ref, rmsg_ref, tmsg_ref, keep_ref, rows, *, galaxy_z):
    count, slab, width = tmpl_ref.shape
    chunks = rmsg_ref.shape[0] // 4
    ivar = ivar_ref[...].astype(F32)
    weighted = (ivar * flux_ref[...].astype(F32)).astype(BF16).astype(F32)
    for core in range(2):
        for which, value in enumerate((ivar, weighted)):
            for s in range(chunks):
                row = (core * 2 + which) * chunks + s
                start = (2 * s + core) * width
                rows[row : row + 1, :] = value[:, start : start + width]
    rmsg_ref[...] = rows[...].astype(BF16)
    zeros = jnp.zeros((count * slab, PAD - width), BF16)
    tile = jnp.concatenate([tmpl_ref[...].reshape(count * slab, width), zeros], axis=1)
    for copy in range(tmsg_ref.shape[0]):
        tmsg_ref[copy] = tile
    zindex = lax.broadcasted_iota(jnp.int32, keep_ref.shape, 1)
    keep_ref[...] = jnp.where((zindex < galaxy_z) | (classes_ref[0] == 1), 1.0, 0.0)


def gram_kernel(rows_ref, tmpl_ref, out_ref, rows, acc, *, slab, count):
    chunks = tmpl_ref.shape[0] // 2
    per = 2 * chunks
    nz, width = rows_ref.shape[1], rows_ref.shape[3]
    npairs = count * (count + 1) // 2
    core, z = lax.axis_index("c"), lax.axis_index("z")
    last = PAD // LANES - 1
    rows[last] = jnp.zeros_like(rows[last])
    for j in range(2):
        for other in range(nz):
            block = rows_ref[j, other, pl.ds(core * per, per), :].astype(F32)
            owner = lax.rem(j + z + other, 2)
            at = pl.ds((owner * nz + other) * per, per)
            for i in range(last + 1):
                part = block[:, i * LANES : min((i + 1) * LANES, width)]
                rows[i, at, 0 : part.shape[1]] = part
    for s in range(chunks):
        stat = []
        for which in range(2):
            value = strided(rows, which * chunks + s, 2 * nz, per)
            stat.append(value.astype(BF16))
        tk = []
        for k in range(count):
            halves = [
                tmpl_ref[2 * s + h, k * slab : (k + 1) * slab, :] for h in range(2)
            ]
            tk.append(jnp.concatenate(halves, axis=0))
        pairs = []
        for k in range(count):
            for l in range(k, count):
                pairs.append(
                    (tk[k].astype(F32) * tk[l].astype(F32)).astype(BF16)
                )
        gram = lax.dot_general(
            jnp.concatenate(pairs, axis=0), stat[0], NT, preferred_element_type=F32
        )
        proj = lax.dot_general(
            jnp.concatenate(tk, axis=0), stat[1], NT, preferred_element_type=F32
        )
        split = npairs * 2 * slab
        if s == 0:
            acc[0:split, 0 : 2 * nz] = gram
            acc[split:, 0 : 2 * nz] = proj
        else:
            acc[0:split, 0 : 2 * nz] += gram
            acc[split:, 0 : 2 * nz] += proj
    ntarget = 2 * nz
    fold = LANES // ntarget
    where = lax.broadcasted_iota(jnp.int32, (slab, LANES), 1) // ntarget
    for h in range(2):
        for g in range(out_ref.shape[1] // slab):
            packed = None
            for q in range(fold):
                e = min(g * fold + q, npairs + count - 1)
                value = acc[(2 * e + h) * slab : (2 * e + h + 1) * slab, :]
                if q:
                    value = pltpu.roll(value, q * ntarget, 1)
                packed = value if q == 0 else jnp.where(where == q, value, packed)
            out_ref[h, g * slab : (g + 1) * slab, :] = packed


def fit_kernel(part_ref, fit_ref, *, slab, count):
    core = lax.axis_index("c")
    ntarget = fit_ref.shape[0]
    fold = LANES // ntarget
    sums = {}

    def entry(e):
        g, q = divmod(e, fold)
        if g not in sums:
            at = pl.ds(g * slab, slab)
            sums[g] = part_ref[0, core, at, :] + part_ref[1, core, at, :]
        return pltpu.roll(sums[g], LANES - q * ntarget, 1) if q else sums[g]

    gram = {}
    for k in range(count):
        for l in range(k, count):
            gram[l, k] = entry(len(gram))
    proj = [entry(len(gram) + k) for k in range(count)]
    fit = None
    for j in range(count):
        inv = lax.rsqrt(gram[j, j])
        column = {i: gram[i, j] * inv for i in range(j + 1, count)}
        solved = proj[j] * inv
        fit = solved * solved if fit is None else fit + solved * solved
        for i in range(j + 1, count):
            for m in range(j + 1, i + 1):
                gram[i, m] = gram[i, m] - column[i] * column[m]
            proj[i] = proj[i] - column[i] * solved
    fit_ref[...] = (fit / count).T[0:ntarget, :]


def drop_kernel(keep_ref, surface_ref, out_ref):
    nsrc, slab = surface_ref.shape
    for i in range(nsrc):
        at = slice(i * slab, (i + 1) * slab)
        value = surface_ref[i : i + 1, :]
        out_ref[:, at] = jnp.where(keep_ref[:, at] > 0.0, value, 0.0)


def body(flux, ivar, templates, classes):
    slab, count, width = templates.shape
    entries = count * (count + 1) // 2 + count
    chunks = flux.shape[1] // width // 2
    total_z = lax.axis_size(GZ) * slab
    fold = LANES // (2 * lax.axis_size("z"))
    groups = -(-entries // fold)
    rmsg, tmsg, keep = pl.pallas_call(
        functools.partial(prep_kernel, galaxy_z=total_z * 3 // 10),
        out_shape=(
            pltpu.VMEM((2 * 2 * chunks, width), BF16),
            pltpu.VMEM((2 * chunks, count * slab, PAD), BF16),
            jax.ShapeDtypeStruct((1, total_z), F32),
        ),
        in_specs=[SMEM] + [VMEM] * 3,
        out_specs=(VMEM, VMEM, VMEM),
        scratch_shapes=[pltpu.VMEM((4 * chunks, width), F32)],
        compiler_params=pltpu.CompilerParams(vmem_limit_bytes=8 << 20),
        name="prep",
    )(classes, in_hbm(flux), in_hbm(ivar), in_hbm(jnp.transpose(templates, (1, 0, 2))))
    tmpl_all = lax.all_to_all(tmsg, PLANE, 0, 0, tiled=True)
    nz = lax.axis_size("z")
    rings = [[(g + z) % 2 * nz + z for z in range(nz)] for g in range(2)]
    ring_rows = lax.all_gather(rmsg, ("c", "z"), axis=0, axis_index_groups=rings)
    rows_all = lax.all_gather(ring_rows, "c", axis=0)
    part = pl.pallas_call(
        functools.partial(gram_kernel, slab=slab, count=count),
        out_shape=pltpu.VMEM((2, groups * slab, LANES), F32),
        in_specs=[VMEM] * 2,
        out_specs=VMEM,
        scratch_shapes=[
            pltpu.VMEM((PAD // LANES, 2 * nz * 2 * chunks, LANES), F32),
            pltpu.VMEM((entries * 2 * slab, LANES), F32),
        ],
        compiler_params=pltpu.CompilerParams(vmem_limit_bytes=16 << 20),
        name="gram",
    )(in_vmem(rows_all), tmpl_all)
    both = lax.all_gather(part, "c", axis=0)
    fit = pl.pallas_call(
        functools.partial(fit_kernel, slab=slab, count=count),
        out_shape=pltpu.VMEM((2 * nz, slab), F32),
        in_specs=[VMEM],
        out_specs=VMEM,
        compiler_params=pltpu.CompilerParams(vmem_limit_bytes=4 << 20),
        name="fit",
    )(in_vmem(both))
    surface = lax.all_to_all(fit, ("c", "z"), 0, 0, tiled=True)
    return pl.pallas_call(
        drop_kernel,
        out_shape=jax.ShapeDtypeStruct((1, total_z), F32),
        in_specs=[VMEM, VMEM],
        out_specs=VMEM,
        compiler_params=pltpu.CompilerParams(vmem_limit_bytes=4 << 20),
        name="drop",
    )(in_vmem(keep), in_vmem(surface))


def solution(mesh):
    fine = Mesh(mesh.devices.reshape(4, 2, 2, 2, 16), ("x", "yl", "c", "yh", "z"))
    return jax.shard_map(
        body,
        mesh=fine,
        in_specs=(
            P(TGT + GZ, None),
            P(TGT + GZ, None),
            P(GZ, None, TGT),
            P(TGT + GZ),
        ),
        out_specs=P(TGT + GZ, None),
        check_vma=False,
    )
```

```python
import functools

import jax
import jax.numpy as jnp
from jax import lax
from jax.experimental import pallas as pl
from jax.experimental.pallas import tpu as pltpu
from jax.sharding import Mesh
from jax.sharding import PartitionSpec as P

BF16 = jnp.bfloat16
F32 = jnp.float32
LANES = 128
PAD = 512
TGT = ("x", "yl", "c")
GZ = ("yh", "z")
PLANE = ("x", "yl", "yh")
VMEM = pl.BlockSpec(memory_space=pltpu.VMEM)
SMEM = pl.BlockSpec(memory_space=pltpu.SMEM)
NT = (((1,), (1,)), ((), ()))


def in_hbm(x):
    return pltpu.with_memory_space_constraint(x, pltpu.HBM)


def in_vmem(x):
    return pltpu.with_memory_space_constraint(x, pltpu.VMEM)


def strided(ref, start, size, stride):
    parts = [ref[j, pl.ds(start, size, stride=stride), :] for j in range(ref.shape[0])]
    return jnp.concatenate(parts, axis=1)


def prep_kernel(classes_ref, flux_ref, ivar_ref, tmpl_ref, rmsg_ref, tmsg_ref, keep_ref, rows, *, galaxy_z):
    count, slab, width = tmpl_ref.shape
    chunks = rmsg_ref.shape[0] // 4
    ivar = ivar_ref[...].astype(F32)
    weighted = (ivar * flux_ref[...].astype(F32)).astype(BF16).astype(F32)
    for core in range(2):
        for which, value in enumerate((ivar, weighted)):
            for s in range(chunks):
                row = (core * 2 + which) * chunks + s
                start = (2 * s + core) * width
                rows[row : row + 1, :] = value[:, start : start + width]
    rmsg_ref[...] = rows[0 : 4 * chunks, :].astype(BF16)
    zeros = jnp.zeros((count * slab, PAD - width), BF16)
    tile = jnp.concatenate([tmpl_ref[...].reshape(count * slab, width), zeros], axis=1)
    for copy in range(tmsg_ref.shape[0]):
        tmsg_ref[copy] = tile
    zindex = lax.broadcasted_iota(jnp.int32, keep_ref.shape, 1)
    keep_ref[...] = jnp.where((zindex < galaxy_z) | (classes_ref[0] == 1), 1.0, 0.0)


def gram_kernel(rows_ref, tmpl_ref, out_ref, ivars, weights, *, slab, count):
    chunks = tmpl_ref.shape[0] // 2
    per = 2 * chunks
    nz, width = rows_ref.shape[1], rows_ref.shape[3]
    core, z = lax.axis_index("c"), lax.axis_index("z")
    last = PAD // LANES - 1
    for ref in (ivars, weights):
        ref[last] = jnp.zeros_like(ref[last])
    for j in range(2):
        for other in range(nz):
            block = rows_ref[j, other, pl.ds(core * per, per), :].astype(F32)
            owner = lax.rem(j + z + other, 2)
            at = pl.ds((owner * nz + other) * chunks, chunks)
            for which, ref in enumerate((ivars, weights)):
                part = block[which * chunks : (which + 1) * chunks]
                for i in range(last + 1):
                    piece = part[:, i * LANES : min((i + 1) * LANES, width)]
                    ref[i, at, 0 : piece.shape[1]] = piece

    def by_chunk(ref):
        parts = [strided(ref, s, 2 * nz, chunks).astype(BF16) for s in range(chunks)]
        return jnp.concatenate(parts, axis=1)

    def template(k):
        at = slice(k * slab, (k + 1) * slab)
        parts = [
            jnp.concatenate([tmpl_ref[2 * s, at, :], tmpl_ref[2 * s + 1, at, :]], axis=0)
            for s in range(chunks)
        ]
        return jnp.concatenate(parts, axis=1)

    def sums(lhs, rhs):
        out = lax.dot_general(
            jnp.concatenate(lhs, axis=0), rhs, NT, preferred_element_type=F32
        )
        return [out[i * 2 * slab : (i + 1) * 2 * slab] for i in range(len(lhs))]

    stat = by_chunk(ivars)
    tk = [template(k) for k in range(count)]
    entries = []
    for k in range(count):
        entries += sums([tk[k] * tk[l] for l in range(k, count)], stat)
    entries += sums(tk, by_chunk(weights))
    fold = LANES // (2 * nz)
    for h in range(2):
        for g in range(out_ref.shape[1] // slab):
            parts = [
                entries[min(e, len(entries) - 1)][h * slab : (h + 1) * slab]
                for e in range(g * fold, (g + 1) * fold)
            ]
            out_ref[h, g * slab : (g + 1) * slab, :] = jnp.concatenate(parts, axis=1)


def fit_kernel(part_ref, fit_ref, *, slab, count):
    core = lax.axis_index("c")
    ntarget = fit_ref.shape[0]
    fold = LANES // ntarget
    sums = {}

    def entry(e):
        g, q = divmod(e, fold)
        if g not in sums:
            at = pl.ds(g * slab, slab)
            sums[g] = part_ref[0, core, at, :] + part_ref[1, core, at, :]
        return pltpu.roll(sums[g], LANES - q * ntarget, 1) if q else sums[g]

    gram = {}
    for k in range(count):
        for l in range(k, count):
            gram[l, k] = entry(len(gram))
    proj = [entry(len(gram) + k) for k in range(count)]
    fit = None
    for j in range(count):
        inv = lax.rsqrt(gram[j, j])
        column = {i: gram[i, j] * inv for i in range(j + 1, count)}
        solved = proj[j] * inv
        fit = solved * solved if fit is None else fit + solved * solved
        for i in range(j + 1, count):
            for m in range(j + 1, i + 1):
                gram[i, m] = gram[i, m] - column[i] * column[m]
            proj[i] = proj[i] - column[i] * solved
    fit_ref[...] = (fit / count).T[0:ntarget, :]


def drop_kernel(keep_ref, surface_ref, out_ref):
    nsrc, slab = surface_ref.shape
    for i in range(nsrc):
        at = slice(i * slab, (i + 1) * slab)
        value = surface_ref[i : i + 1, :]
        out_ref[:, at] = jnp.where(keep_ref[:, at] > 0.0, value, 0.0)


def body(flux, ivar, templates, classes):
    slab, count, width = templates.shape
    entries = count * (count + 1) // 2 + count
    chunks = flux.shape[1] // width // 2
    total_z = lax.axis_size(GZ) * slab
    fold = LANES // (2 * lax.axis_size("z"))
    groups = -(-entries // fold)
    rmsg, tmsg, keep = pl.pallas_call(
        functools.partial(prep_kernel, galaxy_z=total_z * 3 // 10),
        out_shape=(
            pltpu.VMEM((2 * 2 * chunks, width), BF16),
            pltpu.VMEM((2 * chunks, count * slab, PAD), BF16),
            jax.ShapeDtypeStruct((1, total_z), F32),
        ),
        in_specs=[SMEM] + [VMEM] * 3,
        out_specs=(VMEM, VMEM, VMEM),
        scratch_shapes=[pltpu.VMEM((4 * chunks + 8, width), F32)],
        compiler_params=pltpu.CompilerParams(vmem_limit_bytes=8 << 20),
        name="prep",
    )(classes, in_hbm(flux), in_hbm(ivar), in_hbm(jnp.transpose(templates, (1, 0, 2))))
    tmpl_all = lax.all_to_all(tmsg, PLANE, 0, 0, tiled=True)
    nz = lax.axis_size("z")
    rings = [[(g + z) % 2 * nz + z for z in range(nz)] for g in range(2)]
    ring_rows = lax.all_gather(rmsg, ("c", "z"), axis=0, axis_index_groups=rings)
    rows_all = lax.all_gather(ring_rows, "c", axis=0)
    part = pl.pallas_call(
        functools.partial(gram_kernel, slab=slab, count=count),
        out_shape=pltpu.VMEM((2, groups * slab, LANES), F32),
        in_specs=[VMEM] * 2,
        out_specs=VMEM,
        scratch_shapes=[
            pltpu.VMEM((PAD // LANES, (2 * nz + 1) * chunks, LANES), F32),
            pltpu.VMEM((PAD // LANES, (2 * nz + 1) * chunks, LANES), F32),
        ],
        compiler_params=pltpu.CompilerParams(vmem_limit_bytes=24 << 20),
        name="gram",
    )(in_vmem(rows_all), tmpl_all)
    both = lax.all_gather(part, "c", axis=0)
    fit = pl.pallas_call(
        functools.partial(fit_kernel, slab=slab, count=count),
        out_shape=pltpu.VMEM((2 * nz, slab), F32),
        in_specs=[VMEM],
        out_specs=VMEM,
        compiler_params=pltpu.CompilerParams(vmem_limit_bytes=4 << 20),
        name="fit",
    )(in_vmem(both))
    surface = lax.all_to_all(fit, ("c", "z"), 0, 0, tiled=True)
    return pl.pallas_call(
        drop_kernel,
        out_shape=jax.ShapeDtypeStruct((1, total_z), F32),
        in_specs=[VMEM, VMEM],
        out_specs=VMEM,
        compiler_params=pltpu.CompilerParams(vmem_limit_bytes=4 << 20),
        name="drop",
    )(in_vmem(keep), in_vmem(surface))


def solution(mesh):
    fine = Mesh(mesh.devices.reshape(4, 2, 2, 2, 16), ("x", "yl", "c", "yh", "z"))
    return jax.shard_map(
        body,
        mesh=fine,
        in_specs=(
            P(TGT + GZ, None),
            P(TGT + GZ, None),
            P(GZ, None, TGT),
            P(TGT + GZ),
        ),
        out_specs=P(TGT + GZ, None),
        check_vma=False,
    )
```

```python
import functools

import jax
import jax.numpy as jnp
from jax import lax
from jax.experimental import pallas as pl
from jax.experimental.pallas import tpu as pltpu
from jax.sharding import Mesh
from jax.sharding import PartitionSpec as P

BF16 = jnp.bfloat16
F32 = jnp.float32
LANES = 128
PAD = 512
TGT = ("x", "yl", "c")
GZ = ("yh", "z")
PLANE = ("x", "yl", "yh")
VMEM = pl.BlockSpec(memory_space=pltpu.VMEM)
SMEM = pl.BlockSpec(memory_space=pltpu.SMEM)
NT = (((1,), (1,)), ((), ()))


def in_hbm(x):
    return pltpu.with_memory_space_constraint(x, pltpu.HBM)


def in_vmem(x):
    return pltpu.with_memory_space_constraint(x, pltpu.VMEM)


def strided(ref, start, size, stride):
    parts = [ref[j, pl.ds(start, size, stride=stride), :] for j in range(ref.shape[0])]
    return jnp.concatenate(parts, axis=1)


def pack_kernel(flux_ref, ivar_ref, tmpl_ref, pack_ref, rows):
    nrows = pack_ref.shape[0] - tmpl_ref.shape[0]
    width = tmpl_ref.shape[1]
    chunks = nrows // 4
    ivar = ivar_ref[...].astype(F32)
    weighted = (ivar * flux_ref[...].astype(F32)).astype(BF16).astype(F32)
    for half in range(2):
        for which, value in enumerate((ivar, weighted)):
            for s in range(chunks):
                row = (half * 2 + which) * chunks + s
                start = (2 * s + half) * width
                rows[row : row + 1, :] = value[:, start : start + width]
    pack_ref[0:nrows, :] = rows[0:nrows, :].astype(BF16)
    pack_ref[nrows:, :] = tmpl_ref[...]


def send_kernel(classes_ref, both_ref, rmsg_ref, tmsg_ref, keep_ref, *, galaxy_z):
    nrows, width = rmsg_ref.shape
    per = nrows // 2
    ring = lax.rem(lax.axis_index("c") + lax.axis_index("z"), 2)
    for core in range(2):
        rmsg_ref[core * per : (core + 1) * per, :] = both_ref[core, pl.ds(ring * per, per), :]
    tmpl = both_ref[ring, nrows:, :]
    zeros = jnp.zeros((tmpl.shape[0], PAD - width), BF16)
    tile = jnp.concatenate([tmpl, zeros], axis=1)
    for copy in range(tmsg_ref.shape[0]):
        tmsg_ref[copy] = tile
    zindex = lax.broadcasted_iota(jnp.int32, keep_ref.shape, 1)
    keep_ref[...] = jnp.where((zindex < galaxy_z) | (classes_ref[0] == 1), 1.0, 0.0)


def gram_kernel(rows_ref, tmpl_ref, out_ref, ivars, weights, *, slab, count):
    chunks = tmpl_ref.shape[0] // 2
    nz, width = rows_ref.shape[0], rows_ref.shape[2]
    last = PAD // LANES - 1
    for ref in (ivars, weights):
        ref[last] = jnp.zeros_like(ref[last])
    for other in range(nz):
        block = rows_ref[other].astype(F32)
        for core in range(2):
            for which, ref in enumerate((ivars, weights)):
                part = block[(core * 2 + which) * chunks :][:chunks]
                at = (core * nz + other) * chunks
                for i in range(last + 1):
                    piece = part[:, i * LANES : min((i + 1) * LANES, width)]
                    ref[i, at : at + chunks, 0 : piece.shape[1]] = piece

    def by_chunk(ref):
        parts = [strided(ref, s, 2 * nz, chunks).astype(BF16) for s in range(chunks)]
        return jnp.concatenate(parts, axis=1)

    def template(k):
        at = slice(k * slab, (k + 1) * slab)
        parts = [
            jnp.concatenate([tmpl_ref[2 * s, at, :], tmpl_ref[2 * s + 1, at, :]], axis=0)
            for s in range(chunks)
        ]
        return jnp.concatenate(parts, axis=1)

    def sums(lhs, rhs):
        out = lax.dot_general(
            jnp.concatenate(lhs, axis=0), rhs, NT, preferred_element_type=F32
        )
        return [out[i * 2 * slab : (i + 1) * 2 * slab] for i in range(len(lhs))]

    stat = by_chunk(ivars)
    tk = [template(k) for k in range(count)]
    entries = []
    for k in range(count):
        entries += sums([tk[k] * tk[l] for l in range(k, count)], stat)
    entries += sums(tk, by_chunk(weights))
    fold = LANES // (2 * nz)
    for h in range(2):
        for g in range(out_ref.shape[1] // slab):
            parts = [
                entries[min(e, len(entries) - 1)][h * slab : (h + 1) * slab]
                for e in range(g * fold, (g + 1) * fold)
            ]
            out_ref[h, g * slab : (g + 1) * slab, :] = jnp.concatenate(parts, axis=1)


def fit_kernel(part_ref, fit_ref, *, slab, count):
    core = lax.axis_index("c")
    ntarget = fit_ref.shape[0]
    fold = LANES // ntarget
    sums = {}

    def entry(e):
        g, q = divmod(e, fold)
        if g not in sums:
            at = pl.ds(g * slab, slab)
            sums[g] = part_ref[0, core, at, :] + part_ref[1, core, at, :]
        return pltpu.roll(sums[g], LANES - q * ntarget, 1) if q else sums[g]

    gram = {}
    for k in range(count):
        for l in range(k, count):
            gram[l, k] = entry(len(gram))
    proj = [entry(len(gram) + k) for k in range(count)]
    fit = None
    for j in range(count):
        inv = lax.rsqrt(gram[j, j])
        column = {i: gram[i, j] * inv for i in range(j + 1, count)}
        solved = proj[j] * inv
        fit = solved * solved if fit is None else fit + solved * solved
        for i in range(j + 1, count):
            for m in range(j + 1, i + 1):
                gram[i, m] = gram[i, m] - column[i] * column[m]
            proj[i] = proj[i] - column[i] * solved
    fit_ref[...] = (fit / count).T[0:ntarget, :]


def drop_kernel(keep_ref, surface_ref, out_ref):
    nsrc, slab = surface_ref.shape
    for i in range(nsrc):
        at = slice(i * slab, (i + 1) * slab)
        value = surface_ref[i : i + 1, :]
        out_ref[:, at] = jnp.where(keep_ref[:, at] > 0.0, value, 0.0)


def body(flux, ivar, templates, classes):
    slab, count, width = templates.shape
    entries = count * (count + 1) // 2 + count
    chunks = flux.shape[1] // width // 2
    total_z = lax.axis_size(GZ) * slab
    fold = LANES // (2 * lax.axis_size("z"))
    groups = -(-entries // fold)
    nrows = 4 * chunks
    pack = pl.pallas_call(
        pack_kernel,
        out_shape=pltpu.VMEM((nrows + count * slab, width), BF16),
        in_specs=[VMEM] * 3,
        out_specs=VMEM,
        scratch_shapes=[pltpu.VMEM((nrows + 8, width), F32)],
        compiler_params=pltpu.CompilerParams(vmem_limit_bytes=8 << 20),
        name="pack",
    )(
        in_hbm(flux),
        in_hbm(ivar),
        in_hbm(jnp.transpose(templates, (1, 0, 2)).reshape(count * slab, width)),
    )
    both = lax.all_gather(pack, "c", axis=0)
    rmsg, tmsg, keep = pl.pallas_call(
        functools.partial(send_kernel, galaxy_z=total_z * 3 // 10),
        out_shape=(
            pltpu.VMEM((nrows, width), BF16),
            jax.ShapeDtypeStruct((2 * chunks, count * slab, PAD), BF16),
            pltpu.VMEM((1, total_z), F32),
        ),
        in_specs=[SMEM, VMEM],
        out_specs=(VMEM, VMEM, VMEM),
        compiler_params=pltpu.CompilerParams(vmem_limit_bytes=8 << 20),
        name="send",
    )(classes, in_vmem(both))
    tmpl_all = lax.all_to_all(tmsg, PLANE, 0, 0, tiled=True)
    nz = lax.axis_size("z")
    rings = [[(g + z) % 2 * nz + z for z in range(nz)] for g in range(2)]
    rows_all = lax.all_gather(rmsg, ("c", "z"), axis=0, axis_index_groups=rings)
    part = pl.pallas_call(
        functools.partial(gram_kernel, slab=slab, count=count),
        out_shape=pltpu.VMEM((2, groups * slab, LANES), F32),
        in_specs=[VMEM] * 2,
        out_specs=VMEM,
        scratch_shapes=[
            pltpu.VMEM((PAD // LANES, (2 * nz + 1) * chunks, LANES), F32),
            pltpu.VMEM((PAD // LANES, (2 * nz + 1) * chunks, LANES), F32),
        ],
        compiler_params=pltpu.CompilerParams(vmem_limit_bytes=24 << 20),
        name="gram",
    )(in_vmem(rows_all), tmpl_all)
    both = lax.all_gather(part, "c", axis=0)
    fit = pl.pallas_call(
        functools.partial(fit_kernel, slab=slab, count=count),
        out_shape=pltpu.VMEM((2 * nz, slab), F32),
        in_specs=[VMEM],
        out_specs=VMEM,
        compiler_params=pltpu.CompilerParams(vmem_limit_bytes=4 << 20),
        name="fit",
    )(in_vmem(both))
    surface = lax.all_to_all(fit, ("c", "z"), 0, 0, tiled=True)
    return pl.pallas_call(
        drop_kernel,
        out_shape=jax.ShapeDtypeStruct((1, total_z), F32),
        in_specs=[VMEM, VMEM],
        out_specs=VMEM,
        compiler_params=pltpu.CompilerParams(vmem_limit_bytes=4 << 20),
        name="drop",
    )(in_vmem(keep), in_vmem(surface))


def solution(mesh):
    fine = Mesh(mesh.devices.reshape(4, 2, 2, 2, 16), ("x", "yl", "c", "yh", "z"))
    return jax.shard_map(
        body,
        mesh=fine,
        in_specs=(
            P(TGT + GZ, None),
            P(TGT + GZ, None),
            P(GZ, None, TGT),
            P(TGT + GZ),
        ),
        out_specs=P(TGT + GZ, None),
        check_vma=False,
    )
```

```python
import functools

import jax
import jax.numpy as jnp
from jax import lax
from jax.experimental import pallas as pl
from jax.experimental.pallas import tpu as pltpu
from jax.sharding import Mesh
from jax.sharding import PartitionSpec as P

BF16 = jnp.bfloat16
F32 = jnp.float32
LANES = 128
PAD = 512
TGT = ("x", "yl", "c")
GZ = ("yh", "z")
PLANE = ("x", "yl", "yh")
VMEM = pl.BlockSpec(memory_space=pltpu.VMEM)
SMEM = pl.BlockSpec(memory_space=pltpu.SMEM)
NT = (((1,), (1,)), ((), ()))


def in_hbm(x):
    return pltpu.with_memory_space_constraint(x, pltpu.HBM)


def in_vmem(x):
    return pltpu.with_memory_space_constraint(x, pltpu.VMEM)


def strided(ref, start, size, stride):
    parts = [ref[j, pl.ds(start, size, stride=stride), :] for j in range(ref.shape[0])]
    return jnp.concatenate(parts, axis=1)


def pack_kernel(flux_ref, ivar_ref, tmpl_ref, pack_ref, rows):
    nrows = pack_ref.shape[0] - tmpl_ref.shape[0]
    width = tmpl_ref.shape[1]
    chunks = nrows // 4
    ivar = ivar_ref[...].astype(F32)
    weighted = (ivar * flux_ref[...].astype(F32)).astype(BF16).astype(F32)
    for half in range(2):
        for which, value in enumerate((ivar, weighted)):
            for s in range(chunks):
                row = (half * 2 + which) * chunks + s
                start = (2 * s + half) * width
                rows[row : row + 1, :] = value[:, start : start + width]
    pack_ref[0:nrows, :] = rows[0:nrows, :].astype(BF16)
    pack_ref[nrows:, :] = tmpl_ref[...]


def send_kernel(classes_ref, both_ref, rmsg_ref, tmsg_ref, keep_ref, *, galaxy_z):
    nrows, width = rmsg_ref.shape
    per = nrows // 2
    ring = lax.rem(lax.axis_index("c") + lax.axis_index("z"), 2)
    for core in range(2):
        rmsg_ref[core * per : (core + 1) * per, :] = both_ref[core, pl.ds(ring * per, per), :]
    tmpl = both_ref[ring, nrows:, :]
    zeros = jnp.zeros((tmpl.shape[0], PAD - width), BF16)
    tile = jnp.concatenate([tmpl, zeros], axis=1)
    for copy in range(tmsg_ref.shape[0]):
        tmsg_ref[copy] = tile
    zindex = lax.broadcasted_iota(jnp.int32, keep_ref.shape, 1)
    keep_ref[...] = jnp.where((zindex < galaxy_z) | (classes_ref[0] == 1), 1.0, 0.0)


def gram_kernel(rows_ref, tmpl_ref, out_ref, ivars, weights, *, slab, count):
    chunks = tmpl_ref.shape[0] // 2
    nz, width = rows_ref.shape[0], rows_ref.shape[2]
    last = PAD // LANES - 1
    for ref in (ivars, weights):
        ref[last] = jnp.zeros_like(ref[last])
    for other in range(nz):
        block = rows_ref[other].astype(F32)
        for core in range(2):
            for which, ref in enumerate((ivars, weights)):
                part = block[(core * 2 + which) * chunks :][:chunks]
                at = ((core + other) % 2 * nz + other) * chunks
                for i in range(last + 1):
                    piece = part[:, i * LANES : min((i + 1) * LANES, width)]
                    ref[i, at : at + chunks, 0 : piece.shape[1]] = piece

    def by_chunk(ref):
        parts = [strided(ref, s, 2 * nz, chunks).astype(BF16) for s in range(chunks)]
        return jnp.concatenate(parts, axis=1)

    def template(k):
        at = slice(k * slab, (k + 1) * slab)
        parts = [
            jnp.concatenate([tmpl_ref[2 * s, at, :], tmpl_ref[2 * s + 1, at, :]], axis=0)
            for s in range(chunks)
        ]
        return jnp.concatenate(parts, axis=1)

    def sums(lhs, rhs):
        out = lax.dot_general(
            jnp.concatenate(lhs, axis=0), rhs, NT, preferred_element_type=F32
        )
        return [out[i * 2 * slab : (i + 1) * 2 * slab] for i in range(len(lhs))]

    stat = by_chunk(ivars)
    tk = [template(k) for k in range(count)]
    entries = []
    for k in range(count):
        entries += sums([tk[k] * tk[l] for l in range(k, count)], stat)
    entries += sums(tk, by_chunk(weights))
    fold = LANES // nz
    for ring in range(2):
        lanes = slice(ring * nz, (ring + 1) * nz)
        for g in range(out_ref.shape[1] // (2 * slab)):
            parts = [
                entries[min(e, len(entries) - 1)][:, lanes]
                for e in range(g * fold, (g + 1) * fold)
            ]
            at = slice(g * 2 * slab, (g + 1) * 2 * slab)
            out_ref[ring, at, :] = jnp.concatenate(parts, axis=1)


def fit_kernel(part_ref, fit_ref, *, count):
    ring = lax.rem(lax.axis_index("c") + lax.axis_index("z"), 2)
    ntarget, rows = fit_ref.shape
    fold = LANES // ntarget
    sums = {}

    def entry(e):
        g, q = divmod(e, fold)
        if g not in sums:
            at = pl.ds(g * rows, rows)
            sums[g] = part_ref[0, ring, at, :] + part_ref[1, ring, at, :]
        return pltpu.roll(sums[g], LANES - q * ntarget, 1) if q else sums[g]

    gram = {}
    for k in range(count):
        for l in range(k, count):
            gram[l, k] = entry(len(gram))
    proj = [entry(len(gram) + k) for k in range(count)]
    fit = None
    for j in range(count):
        inv = lax.rsqrt(gram[j, j])
        column = {i: gram[i, j] * inv for i in range(j + 1, count)}
        solved = proj[j] * inv
        fit = solved * solved if fit is None else fit + solved * solved
        for i in range(j + 1, count):
            for m in range(j + 1, i + 1):
                gram[i, m] = gram[i, m] - column[i] * column[m]
            proj[i] = proj[i] - column[i] * solved
    fit_ref[...] = (fit / count).T[0:ntarget, :]


def drop_kernel(keep_ref, surface_ref, out_ref):
    nz, rows = surface_ref.shape
    slab = rows // 2
    for half in range(2):
        for z in range(nz):
            at = slice((half * nz + z) * slab, (half * nz + z + 1) * slab)
            value = surface_ref[z : z + 1, half * slab : (half + 1) * slab]
            out_ref[:, at] = jnp.where(keep_ref[:, at] > 0.0, value, 0.0)


def body(flux, ivar, templates, classes):
    slab, count, width = templates.shape
    entries = count * (count + 1) // 2 + count
    chunks = flux.shape[1] // width // 2
    total_z = lax.axis_size(GZ) * slab
    fold = LANES // lax.axis_size("z")
    groups = -(-entries // fold)
    nrows = 4 * chunks
    pack = pl.pallas_call(
        pack_kernel,
        out_shape=pltpu.VMEM((nrows + count * slab, width), BF16),
        in_specs=[VMEM] * 3,
        out_specs=VMEM,
        scratch_shapes=[pltpu.VMEM((nrows + 8, width), F32)],
        compiler_params=pltpu.CompilerParams(vmem_limit_bytes=8 << 20),
        name="pack",
    )(
        in_hbm(flux),
        in_hbm(ivar),
        in_hbm(jnp.transpose(templates, (1, 0, 2)).reshape(count * slab, width)),
    )
    both = lax.all_gather(pack, "c", axis=0)
    rmsg, tmsg, keep = pl.pallas_call(
        functools.partial(send_kernel, galaxy_z=total_z * 3 // 10),
        out_shape=(
            pltpu.VMEM((nrows, width), BF16),
            jax.ShapeDtypeStruct((2 * chunks, count * slab, PAD), BF16),
            pltpu.VMEM((1, total_z), F32),
        ),
        in_specs=[SMEM, VMEM],
        out_specs=(VMEM, VMEM, VMEM),
        compiler_params=pltpu.CompilerParams(vmem_limit_bytes=8 << 20),
        name="send",
    )(classes, in_vmem(both))
    tmpl_all = lax.all_to_all(tmsg, PLANE, 0, 0, tiled=True)
    nz = lax.axis_size("z")
    rings = [[(g + z) % 2 * nz + z for z in range(nz)] for g in range(2)]
    rows_all = lax.all_gather(rmsg, ("c", "z"), axis=0, axis_index_groups=rings)
    part = pl.pallas_call(
        functools.partial(gram_kernel, slab=slab, count=count),
        out_shape=pltpu.VMEM((2, groups * 2 * slab, LANES), F32),
        in_specs=[VMEM] * 2,
        out_specs=VMEM,
        scratch_shapes=[
            pltpu.VMEM((PAD // LANES, (2 * nz + 1) * chunks, LANES), F32),
            pltpu.VMEM((PAD // LANES, (2 * nz + 1) * chunks, LANES), F32),
        ],
        compiler_params=pltpu.CompilerParams(vmem_limit_bytes=24 << 20),
        name="gram",
    )(in_vmem(rows_all), tmpl_all)
    both = lax.all_gather(part, "c", axis=0)
    fit = pl.pallas_call(
        functools.partial(fit_kernel, count=count),
        out_shape=pltpu.VMEM((nz, 2 * slab), F32),
        in_specs=[VMEM],
        out_specs=VMEM,
        compiler_params=pltpu.CompilerParams(vmem_limit_bytes=4 << 20),
        name="fit",
    )(in_vmem(both))
    surface = lax.all_to_all(
        fit, ("c", "z"), 0, 0, tiled=True, axis_index_groups=rings
    )
    return pl.pallas_call(
        drop_kernel,
        out_shape=jax.ShapeDtypeStruct((1, total_z), F32),
        in_specs=[VMEM, VMEM],
        out_specs=VMEM,
        compiler_params=pltpu.CompilerParams(vmem_limit_bytes=4 << 20),
        name="drop",
    )(in_vmem(keep), in_vmem(surface))


def solution(mesh):
    fine = Mesh(mesh.devices.reshape(4, 2, 2, 2, 16), ("x", "yl", "c", "yh", "z"))
    return jax.shard_map(
        body,
        mesh=fine,
        in_specs=(
            P(TGT + GZ, None),
            P(TGT + GZ, None),
            P(GZ, None, TGT),
            P(TGT + GZ),
        ),
        out_specs=P(TGT + GZ, None),
        check_vma=False,
    )
```

```python
import functools

import jax
import jax.numpy as jnp
from jax import lax
from jax.experimental import pallas as pl
from jax.experimental.pallas import tpu as pltpu
from jax.sharding import Mesh
from jax.sharding import PartitionSpec as P

BF16 = jnp.bfloat16
F32 = jnp.float32
LANES = 128
PAD = 512
TGT = ("x", "yl", "c")
GZ = ("yh", "z")
PLANE = ("x", "yl", "yh")
VMEM = pl.BlockSpec(memory_space=pltpu.VMEM)
SMEM = pl.BlockSpec(memory_space=pltpu.SMEM)
NT = (((1,), (1,)), ((), ()))


def in_hbm(x):
    return pltpu.with_memory_space_constraint(x, pltpu.HBM)


def in_vmem(x):
    return pltpu.with_memory_space_constraint(x, pltpu.VMEM)


def strided(ref, start, size, stride):
    parts = [ref[j, pl.ds(start, size, stride=stride), :] for j in range(ref.shape[0])]
    return jnp.concatenate(parts, axis=1)


def pack_kernel(flux_ref, ivar_ref, tmpl_ref, pack_ref, rows):
    nrows = pack_ref.shape[0] - tmpl_ref.shape[0]
    width = tmpl_ref.shape[1]
    chunks = nrows // 4
    ivar = ivar_ref[...].astype(F32)
    weighted = (ivar * flux_ref[...].astype(F32)).astype(BF16).astype(F32)
    for half in range(2):
        for which, value in enumerate((ivar, weighted)):
            for s in range(chunks):
                row = (half * 2 + which) * chunks + s
                start = (2 * s + half) * width
                rows[row : row + 1, :] = value[:, start : start + width]
    pack_ref[0:nrows, :] = rows[0:nrows, :].astype(BF16)
    pack_ref[nrows:, :] = tmpl_ref[...]


def send_kernel(classes_ref, both_ref, rmsg_ref, tmsg_ref, keep_ref, *, galaxy_z):
    nrows, width = rmsg_ref.shape
    per = nrows // 2
    ring = lax.rem(lax.axis_index("c") + lax.axis_index("z"), 2)
    for core in range(2):
        rmsg_ref[core * per : (core + 1) * per, :] = both_ref[core, pl.ds(ring * per, per), :]
    tmpl = both_ref[ring, nrows:, :]
    zeros = jnp.zeros((tmpl.shape[0], PAD - width), BF16)
    tile = jnp.concatenate([tmpl, zeros], axis=1)
    for copy in range(tmsg_ref.shape[0]):
        tmsg_ref[copy] = tile
    zindex = lax.broadcasted_iota(jnp.int32, keep_ref.shape, 1)
    keep_ref[...] = jnp.where((zindex < galaxy_z) | (classes_ref[0] == 1), 1.0, 0.0)


def gram_kernel(rows_ref, tmpl_ref, out_ref, ivars, weights, *, slab, count):
    chunks = tmpl_ref.shape[0] // 2
    nz, width = rows_ref.shape[0], rows_ref.shape[2]
    last = PAD // LANES - 1
    for ref in (ivars, weights):
        ref[last] = jnp.zeros_like(ref[last])
    for other in range(nz):
        block = rows_ref[other].astype(F32)
        for core in range(2):
            for which, ref in enumerate((ivars, weights)):
                part = block[(core * 2 + which) * chunks :][:chunks]
                at = ((core + other) % 2 * nz + other) * chunks
                for i in range(last + 1):
                    piece = part[:, i * LANES : min((i + 1) * LANES, width)]
                    ref[i, at : at + chunks, 0 : piece.shape[1]] = piece

    def by_chunk(ref):
        parts = [strided(ref, s, 2 * nz, chunks).astype(BF16) for s in range(chunks)]
        return jnp.concatenate(parts, axis=1)

    def template(k):
        at = slice(k * slab, (k + 1) * slab)
        parts = [
            jnp.concatenate([tmpl_ref[2 * s, at, :], tmpl_ref[2 * s + 1, at, :]], axis=0)
            for s in range(chunks)
        ]
        return jnp.concatenate(parts, axis=1)

    tk = [template(k) for k in range(count)]
    pairs = [tk[k] * tk[l] for k in range(count) for l in range(k, count)]
    fold = LANES // (2 * slab)
    at = 0
    for lhs, rhs in ((by_chunk(ivars), pairs), (by_chunk(weights), tk)):
        zeros = [jnp.zeros_like(tk[0])] * (-len(rhs) % fold)
        out = lax.dot_general(
            lhs, jnp.concatenate(rhs + zeros, axis=0), NT, preferred_element_type=F32
        )
        for g in range(out.shape[1] // LANES):
            for ring in range(2):
                value = out[ring * nz : (ring + 1) * nz, g * LANES : (g + 1) * LANES]
                out_ref[ring, at : at + nz, :] = value
            at += nz


def fit_kernel(part_ref, fit_ref, *, count):
    ring = lax.rem(lax.axis_index("c") + lax.axis_index("z"), 2)
    ntarget, width = fit_ref.shape
    fold = LANES // width
    npairs = count * (count + 1) // 2
    first_proj = -(-npairs // fold) * fold
    sums = {}

    def entry(e):
        g, q = divmod(e, fold)
        if g not in sums:
            at = pl.ds(g * ntarget, ntarget)
            sums[g] = part_ref[0, ring, at, :] + part_ref[1, ring, at, :]
        return pltpu.roll(sums[g], LANES - q * width, 1) if q else sums[g]

    gram = {}
    for k in range(count):
        for l in range(k, count):
            gram[l, k] = entry(len(gram))
    proj = [entry(first_proj + k) for k in range(count)]
    fit = None
    for j in range(count):
        inv = lax.rsqrt(gram[j, j])
        column = {i: gram[i, j] * inv for i in range(j + 1, count)}
        solved = proj[j] * inv
        fit = solved * solved if fit is None else fit + solved * solved
        for i in range(j + 1, count):
            for m in range(j + 1, i + 1):
                gram[i, m] = gram[i, m] - column[i] * column[m]
            proj[i] = proj[i] - column[i] * solved
    fit_ref[...] = (fit / count)[:, 0:width]


def drop_kernel(keep_ref, surface_ref, out_ref):
    nz, rows = surface_ref.shape
    slab = rows // 2
    for half in range(2):
        for z in range(nz):
            at = slice((half * nz + z) * slab, (half * nz + z + 1) * slab)
            value = surface_ref[z : z + 1, half * slab : (half + 1) * slab]
            out_ref[:, at] = jnp.where(keep_ref[:, at] > 0.0, value, 0.0)


def body(flux, ivar, templates, classes):
    slab, count, width = templates.shape
    chunks = flux.shape[1] // width // 2
    total_z = lax.axis_size(GZ) * slab
    fold = LANES // (2 * slab)
    groups = -(-(count * (count + 1) // 2) // fold) + -(-count // fold)
    nrows = 4 * chunks
    pack = pl.pallas_call(
        pack_kernel,
        out_shape=pltpu.VMEM((nrows + count * slab, width), BF16),
        in_specs=[VMEM] * 3,
        out_specs=VMEM,
        scratch_shapes=[pltpu.VMEM((nrows + 8, width), F32)],
        compiler_params=pltpu.CompilerParams(vmem_limit_bytes=8 << 20),
        name="pack",
    )(
        in_hbm(flux),
        in_hbm(ivar),
        in_hbm(jnp.transpose(templates, (1, 0, 2)).reshape(count * slab, width)),
    )
    both = lax.all_gather(pack, "c", axis=0)
    rmsg, tmsg, keep = pl.pallas_call(
        functools.partial(send_kernel, galaxy_z=total_z * 3 // 10),
        out_shape=(
            pltpu.VMEM((nrows, width), BF16),
            jax.ShapeDtypeStruct((2 * chunks, count * slab, PAD), BF16),
            pltpu.VMEM((1, total_z), F32),
        ),
        in_specs=[SMEM, VMEM],
        out_specs=(VMEM, VMEM, VMEM),
        compiler_params=pltpu.CompilerParams(vmem_limit_bytes=8 << 20),
        name="send",
    )(classes, in_vmem(both))
    tmpl_all = lax.all_to_all(tmsg, PLANE, 0, 0, tiled=True)
    nz = lax.axis_size("z")
    rings = [[(g + z) % 2 * nz + z for z in range(nz)] for g in range(2)]
    rows_all = lax.all_gather(rmsg, ("c", "z"), axis=0, axis_index_groups=rings)
    part = pl.pallas_call(
        functools.partial(gram_kernel, slab=slab, count=count),
        out_shape=pltpu.VMEM((2, groups * lax.axis_size("z"), LANES), F32),
        in_specs=[VMEM] * 2,
        out_specs=VMEM,
        scratch_shapes=[
            pltpu.VMEM((PAD // LANES, (2 * nz + 1) * chunks, LANES), F32),
            pltpu.VMEM((PAD // LANES, (2 * nz + 1) * chunks, LANES), F32),
        ],
        compiler_params=pltpu.CompilerParams(vmem_limit_bytes=24 << 20),
        name="gram",
    )(in_vmem(rows_all), tmpl_all)
    both = lax.all_gather(part, "c", axis=0)
    fit = pl.pallas_call(
        functools.partial(fit_kernel, count=count),
        out_shape=pltpu.VMEM((nz, 2 * slab), F32),
        in_specs=[VMEM],
        out_specs=VMEM,
        compiler_params=pltpu.CompilerParams(vmem_limit_bytes=4 << 20),
        name="fit",
    )(in_vmem(both))
    surface = lax.all_to_all(
        fit, ("c", "z"), 0, 0, tiled=True, axis_index_groups=rings
    )
    return pl.pallas_call(
        drop_kernel,
        out_shape=jax.ShapeDtypeStruct((1, total_z), F32),
        in_specs=[VMEM, VMEM],
        out_specs=VMEM,
        compiler_params=pltpu.CompilerParams(vmem_limit_bytes=4 << 20),
        name="drop",
    )(in_vmem(keep), in_vmem(surface))


def solution(mesh):
    fine = Mesh(mesh.devices.reshape(4, 2, 2, 2, 16), ("x", "yl", "c", "yh", "z"))
    return jax.shard_map(
        body,
        mesh=fine,
        in_specs=(
            P(TGT + GZ, None),
            P(TGT + GZ, None),
            P(GZ, None, TGT),
            P(TGT + GZ),
        ),
        out_specs=P(TGT + GZ, None),
        check_vma=False,
    )
```

```python
import functools

import jax
import jax.numpy as jnp
from jax import lax
from jax.experimental import pallas as pl
from jax.experimental.pallas import tpu as pltpu
from jax.sharding import Mesh
from jax.sharding import PartitionSpec as P

BF16 = jnp.bfloat16
F32 = jnp.float32
LANES = 128
PAD = 512
TGT = ("x", "yl", "c")
GZ = ("yh", "z")
PLANE = ("x", "yl", "yh")
VMEM = pl.BlockSpec(memory_space=pltpu.VMEM)
SMEM = pl.BlockSpec(memory_space=pltpu.SMEM)
NT = (((1,), (1,)), ((), ()))


def in_hbm(x):
    return pltpu.with_memory_space_constraint(x, pltpu.HBM)


def in_vmem(x):
    return pltpu.with_memory_space_constraint(x, pltpu.VMEM)


def strided(ref, start, size, stride):
    parts = [ref[j, pl.ds(start, size, stride=stride), :] for j in range(ref.shape[0])]
    return jnp.concatenate(parts, axis=1)


def pack_kernel(flux_ref, ivar_ref, tmpl_ref, pack_ref, rows):
    nrows = pack_ref.shape[0] - tmpl_ref.shape[0]
    width = tmpl_ref.shape[1]
    chunks = nrows // 4
    ivar = ivar_ref[...].astype(F32)
    weighted = (ivar * flux_ref[...].astype(F32)).astype(BF16).astype(F32)
    for half in range(2):
        for which, value in enumerate((ivar, weighted)):
            for s in range(chunks):
                row = (half * 2 + which) * chunks + s
                start = (2 * s + half) * width
                rows[row : row + 1, :] = value[:, start : start + width]
    pack_ref[0:nrows, :] = rows[0:nrows, :].astype(BF16)
    pack_ref[nrows:, :] = tmpl_ref[...]


def send_kernel(classes_ref, both_ref, rmsg_ref, tmsg_ref, keep_ref, *, galaxy_z):
    nrows, width = rmsg_ref.shape
    per = nrows // 2
    ring = lax.rem(lax.axis_index("c") + lax.axis_index("z"), 2)
    for core in range(2):
        rmsg_ref[core * per : (core + 1) * per, :] = both_ref[core, pl.ds(ring * per, per), :]
    tmpl = both_ref[ring, nrows:, :]
    zeros = jnp.zeros((tmpl.shape[0], PAD - width), BF16)
    tile = jnp.concatenate([tmpl, zeros], axis=1)
    for copy in range(tmsg_ref.shape[0]):
        tmsg_ref[copy] = tile
    zindex = lax.broadcasted_iota(jnp.int32, keep_ref.shape, 1)
    keep_ref[...] = jnp.where((zindex < galaxy_z) | (classes_ref[0] == 1), 1.0, 0.0)


def gram_kernel(rows_ref, tmpl_ref, own_ref, other_ref, ivars, weights, *, slab, count):
    chunks = tmpl_ref.shape[0] // 2
    nz, width = rows_ref.shape[0], rows_ref.shape[2]
    last = PAD // LANES - 1
    for ref in (ivars, weights):
        ref[last] = jnp.zeros_like(ref[last])
    for other in range(nz):
        block = rows_ref[other].astype(F32)
        for core in range(2):
            for which, ref in enumerate((ivars, weights)):
                part = block[(core * 2 + which) * chunks :][:chunks]
                at = ((core + other) % 2 * nz + other) * chunks
                for i in range(last + 1):
                    piece = part[:, i * LANES : min((i + 1) * LANES, width)]
                    ref[i, at : at + chunks, 0 : piece.shape[1]] = piece

    def by_chunk(ref):
        parts = [strided(ref, s, 2 * nz, chunks).astype(BF16) for s in range(chunks)]
        return jnp.concatenate(parts, axis=1)

    def template(k):
        at = slice(k * slab, (k + 1) * slab)
        parts = [
            jnp.concatenate([tmpl_ref[2 * s, at, :], tmpl_ref[2 * s + 1, at, :]], axis=0)
            for s in range(chunks)
        ]
        return jnp.concatenate(parts, axis=1)

    tk = [template(k) for k in range(count)]
    pairs = [tk[k] * tk[l] for k in range(count) for l in range(k, count)]
    first = lax.rem(lax.axis_index("c") + lax.axis_index("z"), 2) == 0
    fold = LANES // (2 * slab)
    at = 0
    for lhs, rhs in ((by_chunk(ivars), pairs), (by_chunk(weights), tk)):
        zeros = [jnp.zeros_like(tk[0])] * (-len(rhs) % fold)
        out = lax.dot_general(
            lhs, jnp.concatenate(rhs + zeros, axis=0), NT, preferred_element_type=F32
        )
        for g in range(out.shape[1] // LANES):
            lanes = slice(g * LANES, (g + 1) * LANES)
            low, high = out[0:nz, lanes], out[nz : 2 * nz, lanes]
            own_ref[at : at + nz, :] = jnp.where(first, low, high)
            other_ref[at : at + nz, :] = jnp.where(first, high, low)
            at += nz


def fit_kernel(own_ref, sent_ref, fit_ref, *, count):
    partner = 1 - lax.axis_index("c")
    ntarget, width = fit_ref.shape
    fold = LANES // width
    npairs = count * (count + 1) // 2
    first_proj = -(-npairs // fold) * fold
    sums = {}

    def entry(e):
        g, q = divmod(e, fold)
        if g not in sums:
            at = pl.ds(g * ntarget, ntarget)
            sums[g] = own_ref[at, :] + sent_ref[partner, at, :]
        return pltpu.roll(sums[g], LANES - q * width, 1) if q else sums[g]

    gram = {}
    for k in range(count):
        for l in range(k, count):
            gram[l, k] = entry(len(gram))
    proj = [entry(first_proj + k) for k in range(count)]
    fit = None
    for j in range(count):
        inv = lax.rsqrt(gram[j, j])
        column = {i: gram[i, j] * inv for i in range(j + 1, count)}
        solved = proj[j] * inv
        fit = solved * solved if fit is None else fit + solved * solved
        for i in range(j + 1, count):
            for m in range(j + 1, i + 1):
                gram[i, m] = gram[i, m] - column[i] * column[m]
            proj[i] = proj[i] - column[i] * solved
    fit_ref[...] = (fit / count)[:, 0:width]


def drop_kernel(keep_ref, surface_ref, out_ref):
    nz, rows = surface_ref.shape
    slab = rows // 2
    for half in range(2):
        for z in range(nz):
            at = slice((half * nz + z) * slab, (half * nz + z + 1) * slab)
            value = surface_ref[z : z + 1, half * slab : (half + 1) * slab]
            out_ref[:, at] = jnp.where(keep_ref[:, at] > 0.0, value, 0.0)


def body(flux, ivar, templates, classes):
    slab, count, width = templates.shape
    chunks = flux.shape[1] // width // 2
    total_z = lax.axis_size(GZ) * slab
    fold = LANES // (2 * slab)
    groups = -(-(count * (count + 1) // 2) // fold) + -(-count // fold)
    nrows = 4 * chunks
    pack = pl.pallas_call(
        pack_kernel,
        out_shape=pltpu.VMEM((nrows + count * slab, width), BF16),
        in_specs=[VMEM] * 3,
        out_specs=VMEM,
        scratch_shapes=[pltpu.VMEM((nrows + 8, width), F32)],
        compiler_params=pltpu.CompilerParams(vmem_limit_bytes=8 << 20),
        name="pack",
    )(
        in_hbm(flux),
        in_hbm(ivar),
        in_hbm(jnp.transpose(templates, (1, 0, 2)).reshape(count * slab, width)),
    )
    both = lax.all_gather(pack, "c", axis=0)
    rmsg, tmsg, keep = pl.pallas_call(
        functools.partial(send_kernel, galaxy_z=total_z * 3 // 10),
        out_shape=(
            pltpu.VMEM((nrows, width), BF16),
            jax.ShapeDtypeStruct((2 * chunks, count * slab, PAD), BF16),
            pltpu.VMEM((1, total_z), F32),
        ),
        in_specs=[SMEM, VMEM],
        out_specs=(VMEM, VMEM, VMEM),
        compiler_params=pltpu.CompilerParams(vmem_limit_bytes=8 << 20),
        name="send",
    )(classes, in_vmem(both))
    tmpl_all = lax.all_to_all(tmsg, PLANE, 0, 0, tiled=True)
    nz = lax.axis_size("z")
    rings = [[(g + z) % 2 * nz + z for z in range(nz)] for g in range(2)]
    rows_all = lax.all_gather(rmsg, ("c", "z"), axis=0, axis_index_groups=rings)
    own, other = pl.pallas_call(
        functools.partial(gram_kernel, slab=slab, count=count),
        out_shape=(pltpu.VMEM((groups * nz, LANES), F32),) * 2,
        in_specs=[VMEM] * 2,
        out_specs=(VMEM, VMEM),
        scratch_shapes=[
            pltpu.VMEM((PAD // LANES, (2 * nz + 1) * chunks, LANES), F32),
            pltpu.VMEM((PAD // LANES, (2 * nz + 1) * chunks, LANES), F32),
        ],
        compiler_params=pltpu.CompilerParams(vmem_limit_bytes=24 << 20),
        name="gram",
    )(in_vmem(rows_all), tmpl_all)
    sent = lax.all_gather(other, "c", axis=0)
    fit = pl.pallas_call(
        functools.partial(fit_kernel, count=count),
        out_shape=pltpu.VMEM((nz, 2 * slab), F32),
        in_specs=[VMEM, VMEM],
        out_specs=VMEM,
        compiler_params=pltpu.CompilerParams(vmem_limit_bytes=4 << 20),
        name="fit",
    )(in_vmem(own), in_vmem(sent))
    surface = lax.all_to_all(
        fit, ("c", "z"), 0, 0, tiled=True, axis_index_groups=rings
    )
    return pl.pallas_call(
        drop_kernel,
        out_shape=jax.ShapeDtypeStruct((1, total_z), F32),
        in_specs=[VMEM, VMEM],
        out_specs=VMEM,
        compiler_params=pltpu.CompilerParams(vmem_limit_bytes=4 << 20),
        name="drop",
    )(in_vmem(keep), in_vmem(surface))


def solution(mesh):
    fine = Mesh(mesh.devices.reshape(4, 2, 2, 2, 16), ("x", "yl", "c", "yh", "z"))
    return jax.shard_map(
        body,
        mesh=fine,
        in_specs=(
            P(TGT + GZ, None),
            P(TGT + GZ, None),
            P(GZ, None, TGT),
            P(TGT + GZ),
        ),
        out_specs=P(TGT + GZ, None),
        check_vma=False,
    )
```

```python
import functools

import jax
import jax.numpy as jnp
from jax import lax
from jax.experimental import pallas as pl
from jax.experimental.pallas import tpu as pltpu
from jax.sharding import Mesh
from jax.sharding import PartitionSpec as P

BF16 = jnp.bfloat16
F32 = jnp.float32
LANES = 128
PAD = 512
TGT = ("x", "yl", "c")
GZ = ("yh", "z")
PLANE = ("x", "yl", "yh")
VMEM = pl.BlockSpec(memory_space=pltpu.VMEM)
SMEM = pl.BlockSpec(memory_space=pltpu.SMEM)
NT = (((1,), (1,)), ((), ()))


def in_hbm(x):
    return pltpu.with_memory_space_constraint(x, pltpu.HBM)


def in_vmem(x):
    return pltpu.with_memory_space_constraint(x, pltpu.VMEM)


def strided(ref, start, size, stride):
    parts = [ref[j, pl.ds(start, size, stride=stride), :] for j in range(ref.shape[0])]
    return jnp.concatenate(parts, axis=1)


def pack_kernel(flux_ref, ivar_ref, tmpl_ref, pack_ref, rows):
    nrows = pack_ref.shape[0] - tmpl_ref.shape[0]
    width = tmpl_ref.shape[1]
    chunks = nrows // 4
    ivar = ivar_ref[...].astype(F32)
    weighted = (ivar * flux_ref[...].astype(F32)).astype(BF16).astype(F32)
    for half in range(2):
        for which, value in enumerate((ivar, weighted)):
            for s in range(chunks):
                row = (half * 2 + which) * chunks + s
                start = (2 * s + half) * width
                rows[row : row + 1, :] = value[:, start : start + width]
    pack_ref[0:nrows, :] = rows[0:nrows, :].astype(BF16)
    pack_ref[nrows:, :] = tmpl_ref[...]


def send_kernel(classes_ref, both_ref, rmsg_ref, tmsg_ref, keep_ref, *, galaxy_z):
    nrows, width = rmsg_ref.shape
    per = nrows // 2
    ring = lax.rem(lax.axis_index("c") + lax.axis_index("z"), 2)
    for core in range(2):
        rmsg_ref[core * per : (core + 1) * per, :] = both_ref[core, pl.ds(ring * per, per), :]
    tmpl = both_ref[ring, nrows:, :]
    zeros = jnp.zeros((tmpl.shape[0], PAD - width), BF16)
    tile = jnp.concatenate([tmpl, zeros], axis=1)
    for copy in range(tmsg_ref.shape[0]):
        tmsg_ref[copy] = tile
    zindex = lax.broadcasted_iota(jnp.int32, keep_ref.shape, 1)
    keep_ref[...] = jnp.where((zindex < galaxy_z) | (classes_ref[0] == 1), 1.0, 0.0)


def gram_kernel(rows_ref, tmpl_ref, out_ref, ivars, weights, *, slab, count):
    chunks = tmpl_ref.shape[0] // 2
    nz, width = rows_ref.shape[0], rows_ref.shape[2]
    last = PAD // LANES - 1
    for ref in (ivars, weights):
        ref[last] = jnp.zeros_like(ref[last])
    for other in range(nz):
        block = rows_ref[other].astype(F32)
        for core in range(2):
            for which, ref in enumerate((ivars, weights)):
                part = block[(core * 2 + which) * chunks :][:chunks]
                at = ((core + other) % 2 * nz + other) * chunks
                for i in range(last + 1):
                    piece = part[:, i * LANES : min((i + 1) * LANES, width)]
                    ref[i, at : at + chunks, 0 : piece.shape[1]] = piece

    def by_chunk(ref):
        parts = [strided(ref, s, 2 * nz, chunks).astype(BF16) for s in range(chunks)]
        return jnp.concatenate(parts, axis=1)

    def template(k):
        at = slice(k * slab, (k + 1) * slab)
        parts = [
            jnp.concatenate([tmpl_ref[2 * s, at, :], tmpl_ref[2 * s + 1, at, :]], axis=0)
            for s in range(chunks)
        ]
        return jnp.concatenate(parts, axis=1)

    tk = [template(k) for k in range(count)]
    pairs = [tk[k] * tk[l] for k in range(count) for l in range(k, count)]
    fold = LANES // (2 * slab)
    at = 0
    for lhs, rhs in ((by_chunk(ivars), pairs), (by_chunk(weights), tk)):
        zeros = [jnp.zeros_like(tk[0])] * (-len(rhs) % fold)
        out = lax.dot_general(
            lhs, jnp.concatenate(rhs + zeros, axis=0), NT, preferred_element_type=F32
        )
        for g in range(out.shape[1] // LANES):
            for ring in range(2):
                value = out[ring * nz : (ring + 1) * nz, g * LANES : (g + 1) * LANES]
                out_ref[ring, at : at + nz, :] = value
            at += nz


def fit_kernel(part_ref, fit_ref, *, count):
    ring = lax.rem(lax.axis_index("c") + lax.axis_index("z"), 2)
    ntarget, width = fit_ref.shape
    fold = LANES // width
    npairs = count * (count + 1) // 2
    first_proj = -(-npairs // fold) * fold
    sums = {}

    def entry(e):
        g, q = divmod(e, fold)
        if g not in sums:
            at = pl.ds(g * ntarget, ntarget)
            sums[g] = part_ref[0, ring, at, :] + part_ref[1, ring, at, :]
        return pltpu.roll(sums[g], LANES - q * width, 1) if q else sums[g]

    gram = {}
    for k in range(count):
        for l in range(k, count):
            gram[l, k] = entry(len(gram))
    proj = [entry(first_proj + k) for k in range(count)]
    fit = None
    for j in range(count):
        inv = lax.rsqrt(gram[j, j])
        column = {i: gram[i, j] * inv for i in range(j + 1, count)}
        solved = proj[j] * inv
        fit = solved * solved if fit is None else fit + solved * solved
        for i in range(j + 1, count):
            for m in range(j + 1, i + 1):
                gram[i, m] = gram[i, m] - column[i] * column[m]
            proj[i] = proj[i] - column[i] * solved
    fit = (fit / count)[:, 0:width]
    middle = ntarget // 2
    fit_ref[0 : ntarget - middle, :] = fit[middle:, :]
    fit_ref[ntarget - middle :, :] = fit[0:middle, :]


def drop_kernel(keep_ref, surface_ref, out_ref):
    nz, rows = surface_ref.shape
    slab = rows // 2
    for half in range(2):
        for z in range(nz):
            at = slice((half * nz + z) * slab, (half * nz + z + 1) * slab)
            row = (z - nz // 2) % nz
            value = surface_ref[row : row + 1, half * slab : (half + 1) * slab]
            out_ref[:, at] = jnp.where(keep_ref[:, at] > 0.0, value, 0.0)


def body(flux, ivar, templates, classes):
    slab, count, width = templates.shape
    chunks = flux.shape[1] // width // 2
    total_z = lax.axis_size(GZ) * slab
    fold = LANES // (2 * slab)
    groups = -(-(count * (count + 1) // 2) // fold) + -(-count // fold)
    nrows = 4 * chunks
    pack = pl.pallas_call(
        pack_kernel,
        out_shape=pltpu.VMEM((nrows + count * slab, width), BF16),
        in_specs=[VMEM] * 3,
        out_specs=VMEM,
        scratch_shapes=[pltpu.VMEM((nrows + 8, width), F32)],
        compiler_params=pltpu.CompilerParams(vmem_limit_bytes=8 << 20),
        name="pack",
    )(
        in_hbm(flux),
        in_hbm(ivar),
        in_hbm(jnp.transpose(templates, (1, 0, 2)).reshape(count * slab, width)),
    )
    both = lax.all_gather(pack, "c", axis=0)
    rmsg, tmsg, keep = pl.pallas_call(
        functools.partial(send_kernel, galaxy_z=total_z * 3 // 10),
        out_shape=(
            pltpu.VMEM((nrows, width), BF16),
            jax.ShapeDtypeStruct((2 * chunks, count * slab, PAD), BF16),
            pltpu.VMEM((1, total_z), F32),
        ),
        in_specs=[SMEM, VMEM],
        out_specs=(VMEM, VMEM, VMEM),
        compiler_params=pltpu.CompilerParams(vmem_limit_bytes=8 << 20),
        name="send",
    )(classes, in_vmem(both))
    tmpl_all = lax.all_to_all(tmsg, PLANE, 0, 0, tiled=True)
    nz = lax.axis_size("z")
    rings = [[(g + z) % 2 * nz + z for z in range(nz)] for g in range(2)]
    rows_all = lax.all_gather(rmsg, ("c", "z"), axis=0, axis_index_groups=rings)
    part = pl.pallas_call(
        functools.partial(gram_kernel, slab=slab, count=count),
        out_shape=pltpu.VMEM((2, groups * lax.axis_size("z"), LANES), F32),
        in_specs=[VMEM] * 2,
        out_specs=VMEM,
        scratch_shapes=[
            pltpu.VMEM((PAD // LANES, (2 * nz + 1) * chunks, LANES), F32),
            pltpu.VMEM((PAD // LANES, (2 * nz + 1) * chunks, LANES), F32),
        ],
        compiler_params=pltpu.CompilerParams(vmem_limit_bytes=24 << 20),
        name="gram",
    )(in_vmem(rows_all), tmpl_all)
    both = lax.all_gather(part, "c", axis=0)
    fit = pl.pallas_call(
        functools.partial(fit_kernel, count=count),
        out_shape=pltpu.VMEM((nz, 2 * slab), F32),
        in_specs=[VMEM],
        out_specs=VMEM,
        compiler_params=pltpu.CompilerParams(vmem_limit_bytes=4 << 20),
        name="fit",
    )(in_vmem(both))
    turned = [ring[nz // 2 :] + ring[: nz // 2] for ring in rings]
    surface = lax.all_to_all(
        fit, ("c", "z"), 0, 0, tiled=True, axis_index_groups=turned
    )
    return pl.pallas_call(
        drop_kernel,
        out_shape=jax.ShapeDtypeStruct((1, total_z), F32),
        in_specs=[VMEM, VMEM],
        out_specs=VMEM,
        compiler_params=pltpu.CompilerParams(vmem_limit_bytes=4 << 20),
        name="drop",
    )(in_vmem(keep), in_vmem(surface))


def solution(mesh):
    fine = Mesh(mesh.devices.reshape(4, 2, 2, 2, 16), ("x", "yl", "c", "yh", "z"))
    return jax.shard_map(
        body,
        mesh=fine,
        in_specs=(
            P(TGT + GZ, None),
            P(TGT + GZ, None),
            P(GZ, None, TGT),
            P(TGT + GZ),
        ),
        out_specs=P(TGT + GZ, None),
        check_vma=False,
    )
```

```python
import functools

import jax
import jax.numpy as jnp
from jax import lax
from jax.experimental import pallas as pl
from jax.experimental.pallas import tpu as pltpu
from jax.sharding import Mesh
from jax.sharding import PartitionSpec as P

BF16 = jnp.bfloat16
F32 = jnp.float32
LANES = 128
PAD = 512
TGT = ("x", "yl", "c")
GZ = ("yh", "z")
PLANE = ("x", "yl", "yh")
VMEM = pl.BlockSpec(memory_space=pltpu.VMEM)
SMEM = pl.BlockSpec(memory_space=pltpu.SMEM)
NT = (((1,), (1,)), ((), ()))


def in_hbm(x):
    return pltpu.with_memory_space_constraint(x, pltpu.HBM)


def in_vmem(x):
    return pltpu.with_memory_space_constraint(x, pltpu.VMEM)


def strided(ref, start, size, stride):
    parts = [ref[j, pl.ds(start, size, stride=stride), :] for j in range(ref.shape[0])]
    return jnp.concatenate(parts, axis=1)


def pack_kernel(flux_ref, ivar_ref, tmpl_ref, pack_ref, rows):
    nrows = pack_ref.shape[0] - tmpl_ref.shape[0]
    width = tmpl_ref.shape[1]
    chunks = nrows // 4
    ivar = ivar_ref[...].astype(F32)
    weighted = (ivar * flux_ref[...].astype(F32)).astype(BF16).astype(F32)
    for half in range(2):
        for which, value in enumerate((ivar, weighted)):
            for s in range(chunks):
                row = (half * 2 + which) * chunks + s
                start = (2 * s + half) * width
                rows[row : row + 1, :] = value[:, start : start + width]
    pack_ref[0:nrows, :] = rows[0:nrows, :].astype(BF16)
    pack_ref[nrows:, :] = tmpl_ref[...]


def send_kernel(classes_ref, both_ref, rmsg_ref, tmsg_ref, keep_ref, *, galaxy_z):
    nrows, width = rmsg_ref.shape
    per = nrows // 2
    ring = lax.rem(lax.axis_index("c") + lax.axis_index("z"), 2)
    for core in range(2):
        rmsg_ref[core * per : (core + 1) * per, :] = both_ref[core, pl.ds(ring * per, per), :]
    tmpl = both_ref[ring, nrows:, :]
    zeros = jnp.zeros((tmpl.shape[0], PAD - width), BF16)
    tile = jnp.concatenate([tmpl, zeros], axis=1)
    for copy in range(tmsg_ref.shape[0]):
        tmsg_ref[copy] = tile
    zindex = lax.broadcasted_iota(jnp.int32, keep_ref.shape, 1)
    keep_ref[...] = jnp.where((zindex < galaxy_z) | (classes_ref[0] == 1), 1.0, 0.0)


def gram_kernel(rows_ref, tmpl_ref, own_ref, other_ref, ivars, weights, *, slab, count):
    chunks = tmpl_ref.shape[0] // 2
    nz, width = rows_ref.shape[0], rows_ref.shape[2]
    last = PAD // LANES - 1
    for ref in (ivars, weights):
        ref[last] = jnp.zeros_like(ref[last])
    for other in range(nz):
        block = rows_ref[other].astype(F32)
        for core in range(2):
            for which, ref in enumerate((ivars, weights)):
                part = block[(core * 2 + which) * chunks :][:chunks]
                at = ((core + other) % 2 * nz + other) * chunks
                for i in range(last + 1):
                    piece = part[:, i * LANES : min((i + 1) * LANES, width)]
                    ref[i, at : at + chunks, 0 : piece.shape[1]] = piece

    def by_chunk(ref):
        parts = [strided(ref, s, 2 * nz, chunks).astype(BF16) for s in range(chunks)]
        return jnp.concatenate(parts, axis=1)

    def template(k):
        at = slice(k * slab, (k + 1) * slab)
        parts = [
            jnp.concatenate([tmpl_ref[2 * s, at, :], tmpl_ref[2 * s + 1, at, :]], axis=0)
            for s in range(chunks)
        ]
        return jnp.concatenate(parts, axis=1)

    tk = [template(k) for k in range(count)]
    pairs = [tk[k] * tk[l] for k in range(count) for l in range(k, count)]
    first = lax.rem(lax.axis_index("c") + lax.axis_index("z"), 2) == 0
    fold = LANES // (2 * slab)
    at = 0
    for lhs, rhs in ((by_chunk(ivars), pairs), (by_chunk(weights), tk)):
        zeros = [jnp.zeros_like(tk[0])] * (-len(rhs) % fold)
        out = lax.dot_general(
            lhs, jnp.concatenate(rhs + zeros, axis=0), NT, preferred_element_type=F32
        )
        for g in range(out.shape[1] // LANES):
            lanes = slice(g * LANES, (g + 1) * LANES)
            low, high = out[0:nz, lanes], out[nz : 2 * nz, lanes]
            own_ref[at : at + nz, :] = jnp.where(first, low, high)
            other_ref[at : at + nz, :] = jnp.where(first, high, low)
            at += nz


def fit_kernel(own_ref, sent_ref, fit_ref, *, count):
    partner = 1 - lax.axis_index("c")
    ntarget, width = fit_ref.shape
    fold = LANES // width
    npairs = count * (count + 1) // 2
    first_proj = -(-npairs // fold) * fold
    sums = {}

    def entry(e):
        g, q = divmod(e, fold)
        if g not in sums:
            at = pl.ds(g * ntarget, ntarget)
            sums[g] = own_ref[at, :] + sent_ref[partner, at, :]
        return pltpu.roll(sums[g], LANES - q * width, 1) if q else sums[g]

    gram = {}
    for k in range(count):
        for l in range(k, count):
            gram[l, k] = entry(len(gram))
    proj = [entry(first_proj + k) for k in range(count)]
    fit = None
    for j in range(count):
        inv = lax.rsqrt(gram[j, j])
        column = {i: gram[i, j] * inv for i in range(j + 1, count)}
        solved = proj[j] * inv
        fit = solved * solved if fit is None else fit + solved * solved
        for i in range(j + 1, count):
            for m in range(j + 1, i + 1):
                gram[i, m] = gram[i, m] - column[i] * column[m]
            proj[i] = proj[i] - column[i] * solved
    fit = (fit / count)[:, 0:width]
    middle = ntarget // 2
    fit_ref[0 : ntarget - middle, :] = fit[middle:, :]
    fit_ref[ntarget - middle :, :] = fit[0:middle, :]


def drop_kernel(keep_ref, surface_ref, out_ref):
    nz, rows = surface_ref.shape
    slab = rows // 2
    for half in range(2):
        for z in range(nz):
            at = slice((half * nz + z) * slab, (half * nz + z + 1) * slab)
            row = (z - nz // 2) % nz
            value = surface_ref[row : row + 1, half * slab : (half + 1) * slab]
            out_ref[:, at] = jnp.where(keep_ref[:, at] > 0.0, value, 0.0)


def body(flux, ivar, templates, classes):
    slab, count, width = templates.shape
    chunks = flux.shape[1] // width // 2
    total_z = lax.axis_size(GZ) * slab
    fold = LANES // (2 * slab)
    groups = -(-(count * (count + 1) // 2) // fold) + -(-count // fold)
    nrows = 4 * chunks
    pack = pl.pallas_call(
        pack_kernel,
        out_shape=pltpu.VMEM((nrows + count * slab, width), BF16),
        in_specs=[VMEM] * 3,
        out_specs=VMEM,
        scratch_shapes=[pltpu.VMEM((nrows + 8, width), F32)],
        compiler_params=pltpu.CompilerParams(vmem_limit_bytes=8 << 20),
        name="pack",
    )(
        in_hbm(flux),
        in_hbm(ivar),
        in_hbm(jnp.transpose(templates, (1, 0, 2)).reshape(count * slab, width)),
    )
    both = lax.all_gather(pack, "c", axis=0)
    rmsg, tmsg, keep = pl.pallas_call(
        functools.partial(send_kernel, galaxy_z=total_z * 3 // 10),
        out_shape=(
            pltpu.VMEM((nrows, width), BF16),
            jax.ShapeDtypeStruct((2 * chunks, count * slab, PAD), BF16),
            pltpu.VMEM((1, total_z), F32),
        ),
        in_specs=[SMEM, VMEM],
        out_specs=(VMEM, VMEM, VMEM),
        compiler_params=pltpu.CompilerParams(vmem_limit_bytes=8 << 20),
        name="send",
    )(classes, in_vmem(both))
    tmpl_all = lax.all_to_all(tmsg, PLANE, 0, 0, tiled=True)
    nz = lax.axis_size("z")
    rings = [[(g + z) % 2 * nz + z for z in range(nz)] for g in range(2)]
    rows_all = lax.all_gather(rmsg, ("c", "z"), axis=0, axis_index_groups=rings)
    own, other = pl.pallas_call(
        functools.partial(gram_kernel, slab=slab, count=count),
        out_shape=(pltpu.VMEM((groups * nz, LANES), F32),) * 2,
        in_specs=[VMEM] * 2,
        out_specs=(VMEM, VMEM),
        scratch_shapes=[
            pltpu.VMEM((PAD // LANES, (2 * nz + 1) * chunks, LANES), F32),
            pltpu.VMEM((PAD // LANES, (2 * nz + 1) * chunks, LANES), F32),
        ],
        compiler_params=pltpu.CompilerParams(vmem_limit_bytes=24 << 20),
        name="gram",
    )(in_vmem(rows_all), tmpl_all)
    sent = lax.all_gather(other, "c", axis=0)
    fit = pl.pallas_call(
        functools.partial(fit_kernel, count=count),
        out_shape=pltpu.VMEM((nz, 2 * slab), F32),
        in_specs=[VMEM, VMEM],
        out_specs=VMEM,
        compiler_params=pltpu.CompilerParams(vmem_limit_bytes=4 << 20),
        name="fit",
    )(in_vmem(own), in_vmem(sent))
    turned = [ring[nz // 2 :] + ring[: nz // 2] for ring in rings]
    surface = lax.all_to_all(
        fit, ("c", "z"), 0, 0, tiled=True, axis_index_groups=turned
    )
    return pl.pallas_call(
        drop_kernel,
        out_shape=jax.ShapeDtypeStruct((1, total_z), F32),
        in_specs=[VMEM, VMEM],
        out_specs=VMEM,
        compiler_params=pltpu.CompilerParams(vmem_limit_bytes=4 << 20),
        name="drop",
    )(in_vmem(keep), in_vmem(surface))


def solution(mesh):
    fine = Mesh(mesh.devices.reshape(4, 2, 2, 2, 16), ("x", "yl", "c", "yh", "z"))
    return jax.shard_map(
        body,
        mesh=fine,
        in_specs=(
            P(TGT + GZ, None),
            P(TGT + GZ, None),
            P(GZ, None, TGT),
            P(TGT + GZ),
        ),
        out_specs=P(TGT + GZ, None),
        check_vma=False,
    )
```

```python
import functools

import jax
import jax.numpy as jnp
from jax import lax
from jax.experimental import pallas as pl
from jax.experimental.pallas import tpu as pltpu
from jax.sharding import Mesh
from jax.sharding import PartitionSpec as P

BF16 = jnp.bfloat16
F32 = jnp.float32
LANES = 128
PAD = 512
TGT = ("x", "yl", "c")
GZ = ("yh", "z")
PLANE = ("x", "yl", "yh")
VMEM = pl.BlockSpec(memory_space=pltpu.VMEM)
SMEM = pl.BlockSpec(memory_space=pltpu.SMEM)
NT = (((1,), (1,)), ((), ()))


def in_hbm(x):
    return pltpu.with_memory_space_constraint(x, pltpu.HBM)


def in_vmem(x):
    return pltpu.with_memory_space_constraint(x, pltpu.VMEM)


def strided(ref, start, size, stride):
    parts = [ref[j, pl.ds(start, size, stride=stride), :] for j in range(ref.shape[0])]
    return jnp.concatenate(parts, axis=1)


def pack_kernel(flux_ref, ivar_ref, tmpl_ref, pack_ref, rows):
    nrows = pack_ref.shape[0] - tmpl_ref.shape[0]
    width = tmpl_ref.shape[1]
    chunks = nrows // 4
    ivar = ivar_ref[...].astype(F32)
    weighted = (ivar * flux_ref[...].astype(F32)).astype(BF16).astype(F32)
    for half in range(2):
        for which, value in enumerate((ivar, weighted)):
            for s in range(chunks):
                row = (half * 2 + which) * chunks + s
                start = (2 * s + half) * width
                rows[row : row + 1, :] = value[:, start : start + width]
    pack_ref[0:nrows, :] = rows[0:nrows, :].astype(BF16)
    pack_ref[nrows:, :] = tmpl_ref[...]


def send_kernel(classes_ref, both_ref, rmsg_ref, tmsg_ref, keep_ref, *, galaxy_z):
    nrows, width = rmsg_ref.shape
    per = nrows // 2
    ring = lax.rem(lax.axis_index("c") + lax.axis_index("z"), 2)
    for core in range(2):
        rmsg_ref[core * per : (core + 1) * per, :] = both_ref[core, pl.ds(ring * per, per), :]
    tmpl = both_ref[ring, nrows:, :]
    zeros = jnp.zeros((tmpl.shape[0], PAD - width), BF16)
    tile = jnp.concatenate([tmpl, zeros], axis=1)
    for copy in range(tmsg_ref.shape[0]):
        tmsg_ref[copy] = tile
    zindex = lax.broadcasted_iota(jnp.int32, keep_ref.shape, 1)
    keep_ref[...] = jnp.where((zindex < galaxy_z) | (classes_ref[0] == 1), 1.0, 0.0)


def gram_kernel(rows_ref, tmpl_ref, own_ref, other_ref, ivars, weights, *, slab, count):
    chunks = tmpl_ref.shape[0] // 2
    nz, width = rows_ref.shape[0], rows_ref.shape[2]
    last = PAD // LANES - 1
    for ref in (ivars, weights):
        ref[last] = jnp.zeros_like(ref[last])
    for other in range(nz):
        block = rows_ref[other].astype(F32)
        for core in range(2):
            for which, ref in enumerate((ivars, weights)):
                part = block[(core * 2 + which) * chunks :][:chunks]
                at = ((core + other) % 2 * nz + other) * chunks
                for i in range(last + 1):
                    piece = part[:, i * LANES : min((i + 1) * LANES, width)]
                    ref[i, at : at + chunks, 0 : piece.shape[1]] = piece

    def by_chunk(ref):
        parts = [strided(ref, s, 2 * nz, chunks).astype(BF16) for s in range(chunks)]
        return jnp.concatenate(parts, axis=1)

    def template(k):
        at = slice(k * slab, (k + 1) * slab)
        parts = [
            jnp.concatenate([tmpl_ref[2 * s, at, :], tmpl_ref[2 * s + 1, at, :]], axis=0)
            for s in range(chunks)
        ]
        return jnp.concatenate(parts, axis=1)

    tk = [template(k) for k in range(count)]
    pairs = [tk[k] * tk[l] for k in range(count) for l in range(k, count)]
    first = lax.rem(lax.axis_index("c") + lax.axis_index("z"), 2) == 0
    fold = LANES // (2 * slab)
    at = 0
    for lhs, rhs in ((by_chunk(ivars), pairs), (by_chunk(weights), tk)):
        zeros = [jnp.zeros_like(tk[0])] * (len(rhs) % 2)
        out = lax.dot_general(
            lhs, jnp.concatenate(rhs + zeros, axis=0), NT, preferred_element_type=F32
        )
        for g in range(-(-out.shape[1] // LANES)):
            lanes = slice(g * LANES, min((g + 1) * LANES, out.shape[1]))
            size = lanes.stop - lanes.start
            low, high = out[0:nz, lanes], out[nz : 2 * nz, lanes]
            own_ref[at : at + nz, 0:size] = jnp.where(first, low, high)
            other_ref[at : at + nz, 0:size] = jnp.where(first, high, low)
            at += nz


def fit_kernel(own_ref, sent_ref, fit_ref, *, count):
    partner = 1 - lax.axis_index("c")
    ntarget, width = fit_ref.shape
    fold = LANES // width
    npairs = count * (count + 1) // 2
    first_proj = -(-npairs // fold) * fold
    sums = {}

    def entry(e):
        g, q = divmod(e, fold)
        if g not in sums:
            at = pl.ds(g * ntarget, ntarget)
            sums[g] = own_ref[at, :] + sent_ref[partner, at, :]
        return pltpu.roll(sums[g], LANES - q * width, 1) if q else sums[g]

    gram = {}
    for k in range(count):
        for l in range(k, count):
            gram[l, k] = entry(len(gram))
    proj = [entry(first_proj + k) for k in range(count)]
    fit = None
    for j in range(count):
        inv = lax.rsqrt(gram[j, j])
        column = {i: gram[i, j] * inv for i in range(j + 1, count)}
        solved = proj[j] * inv
        fit = solved * solved if fit is None else fit + solved * solved
        for i in range(j + 1, count):
            for m in range(j + 1, i + 1):
                gram[i, m] = gram[i, m] - column[i] * column[m]
            proj[i] = proj[i] - column[i] * solved
    fit = (fit / count)[:, 0:width]
    middle = ntarget // 2
    fit_ref[0 : ntarget - middle, :] = fit[middle:, :]
    fit_ref[ntarget - middle :, :] = fit[0:middle, :]


def drop_kernel(keep_ref, surface_ref, out_ref):
    nz, rows = surface_ref.shape
    slab = rows // 2
    for half in range(2):
        for z in range(nz):
            at = slice((half * nz + z) * slab, (half * nz + z + 1) * slab)
            row = (z - nz // 2) % nz
            value = surface_ref[row : row + 1, half * slab : (half + 1) * slab]
            out_ref[:, at] = jnp.where(keep_ref[:, at] > 0.0, value, 0.0)


def body(flux, ivar, templates, classes):
    slab, count, width = templates.shape
    chunks = flux.shape[1] // width // 2
    total_z = lax.axis_size(GZ) * slab
    fold = LANES // (2 * slab)
    groups = -(-(count * (count + 1) // 2) // fold) + -(-count // fold)
    nrows = 4 * chunks
    pack = pl.pallas_call(
        pack_kernel,
        out_shape=pltpu.VMEM((nrows + count * slab, width), BF16),
        in_specs=[VMEM] * 3,
        out_specs=VMEM,
        scratch_shapes=[pltpu.VMEM((nrows + 8, width), F32)],
        compiler_params=pltpu.CompilerParams(vmem_limit_bytes=8 << 20),
        name="pack",
    )(
        in_hbm(flux),
        in_hbm(ivar),
        in_hbm(jnp.transpose(templates, (1, 0, 2)).reshape(count * slab, width)),
    )
    both = lax.all_gather(pack, "c", axis=0)
    rmsg, tmsg, keep = pl.pallas_call(
        functools.partial(send_kernel, galaxy_z=total_z * 3 // 10),
        out_shape=(
            pltpu.VMEM((nrows, width), BF16),
            jax.ShapeDtypeStruct((2 * chunks, count * slab, PAD), BF16),
            pltpu.VMEM((1, total_z), F32),
        ),
        in_specs=[SMEM, VMEM],
        out_specs=(VMEM, VMEM, VMEM),
        compiler_params=pltpu.CompilerParams(vmem_limit_bytes=8 << 20),
        name="send",
    )(classes, in_vmem(both))
    tmpl_all = lax.all_to_all(tmsg, PLANE, 0, 0, tiled=True)
    nz = lax.axis_size("z")
    rings = [[(g + z) % 2 * nz + z for z in range(nz)] for g in range(2)]
    rows_all = lax.all_gather(rmsg, ("c", "z"), axis=0, axis_index_groups=rings)
    own, other = pl.pallas_call(
        functools.partial(gram_kernel, slab=slab, count=count),
        out_shape=(pltpu.VMEM((groups * nz, LANES), F32),) * 2,
        in_specs=[VMEM] * 2,
        out_specs=(VMEM, VMEM),
        scratch_shapes=[
            pltpu.VMEM((PAD // LANES, (2 * nz + 1) * chunks, LANES), F32),
            pltpu.VMEM((PAD // LANES, (2 * nz + 1) * chunks, LANES), F32),
        ],
        compiler_params=pltpu.CompilerParams(vmem_limit_bytes=24 << 20),
        name="gram",
    )(in_vmem(rows_all), tmpl_all)
    sent = lax.all_gather(other, "c", axis=0)
    fit = pl.pallas_call(
        functools.partial(fit_kernel, count=count),
        out_shape=pltpu.VMEM((nz, 2 * slab), F32),
        in_specs=[VMEM, VMEM],
        out_specs=VMEM,
        compiler_params=pltpu.CompilerParams(vmem_limit_bytes=4 << 20),
        name="fit",
    )(in_vmem(own), in_vmem(sent))
    turned = [ring[nz // 2 :] + ring[: nz // 2] for ring in rings]
    surface = lax.all_to_all(
        fit, ("c", "z"), 0, 0, tiled=True, axis_index_groups=turned
    )
    return pl.pallas_call(
        drop_kernel,
        out_shape=jax.ShapeDtypeStruct((1, total_z), F32),
        in_specs=[VMEM, VMEM],
        out_specs=VMEM,
        compiler_params=pltpu.CompilerParams(vmem_limit_bytes=4 << 20),
        name="drop",
    )(in_vmem(keep), in_vmem(surface))


def solution(mesh):
    fine = Mesh(mesh.devices.reshape(4, 2, 2, 2, 16), ("x", "yl", "c", "yh", "z"))
    return jax.shard_map(
        body,
        mesh=fine,
        in_specs=(
            P(TGT + GZ, None),
            P(TGT + GZ, None),
            P(GZ, None, TGT),
            P(TGT + GZ),
        ),
        out_specs=P(TGT + GZ, None),
        check_vma=False,
    )
```
